512 devices in a mesh: sub: 64 (over z_lo, y, core), strip: 8 (over x, z_hi).
Axes of the slice: x: 4, y: 4, z: 16 (z_hi: 2, z_lo: 8; z = z_hi * 8 + z_lo), core: 2. Of those that a mesh axis runs over, the one named last changes fastest.
Arguments:
- spectra: bfloat16 [128, 256, 2048], P('sub', 'strip'), may hold values from -6 to 6
- offsets: int32 [128], P('sub'), may hold values from 0 to 1023
Outputs:
- foreground: float32 [1024, 256, 128], P('strip', 'sub')
The draws below stay inside these ranges and needn't reach their ends.
All inputs are finite; a program needn't handle non-finite values.
Results may differ from the reference program's by a relative error of at most 0.0068.
Values may be sent and summed in bfloat16 or wider, within the bound.
No kernel may reach another device: no remote copies, remote signals or barrier semaphores. Data moves between devices by JAX's collectives and lax.ppermute only.
A program may use at most 64 MiB of HBM per device.

```python
import math
import jax
import jax.numpy as jnp
from jax import lax

KR = 256
KA = 1024
ROWS = 1024
COLS = 256
WIN = 8
BG = 16
SUBAP = 128


def set_ends(entries, own_key, smallest, largest):
    longest = entries.shape.index(max(entries.shape))
    spots = []
    for shift in (0, 1):
        where = [jax.random.randint(jax.random.fold_in(own_key, axis), (), 0, length) for axis, length in enumerate(entries.shape)]
        where[longest] = (where[longest] + shift) % entries.shape[longest]
        spots.append(tuple(where))
    return entries.at[spots[0]].set(smallest).at[spots[1]].set(largest)


def steps_of(key, shape, pieces, low, largest):
    level, own = 1.0, jax.random.fold_in(key, 6)
    for axis_at, blocks in pieces:
        draws = jnp.exp(jax.random.uniform(jax.random.fold_in(own, axis_at), (blocks,), jnp.float32, low / len(pieces), largest / len(pieces)))
        level = level * jnp.repeat(draws, shape[axis_at] // blocks).reshape([-1 if axis == axis_at else 1 for axis in range(len(shape))])
    return level


def gaussian(stream_key, dims, scale, bound, cuts=(), held_as=jnp.bfloat16):
    result = jax.random.normal(stream_key, dims, jnp.float32) * scale
    if len(cuts) > 0:
        result = steps_of(stream_key, dims, cuts, -0.22, 0.18) * result
    return jnp.clip(result, min=-bound, max=bound).astype(held_as)


def setup_inputs(seed: int = 0) -> dict:
    keys = jax.random.split(jax.random.key(seed), 3)
    return {
        "spectra": gaussian(keys[0], (SUBAP, KR, 2 * KA), 1.0, 6.0, ((0, 64), (1, 8))),
        "offsets": set_ends(jax.random.randint(keys[1], (SUBAP,), 0, ROWS), jax.random.fold_in(keys[1], 1), 0, ROWS - 1).astype(jnp.int32),
    }


def column_table(samples, width):
    sample_index = jnp.arange(samples, dtype=jnp.int32)[:, None]
    column_index = jnp.arange(width, dtype=jnp.int32)[None, :]
    phase = jnp.mod(sample_index * column_index, samples).astype(jnp.float32) * (2.0 * math.pi / samples)
    cosine = jnp.cos(phase) / math.sqrt(samples)
    sine = -jnp.sin(phase) / math.sqrt(samples)
    upper = jnp.concatenate([cosine, sine], axis=1)
    lower = jnp.concatenate([-sine, cosine], axis=1)
    return jnp.concatenate([upper, lower], axis=0).astype(jnp.bfloat16)

def row_table(row_index, samples, image_rows):
    sample_index = jnp.arange(samples, dtype=jnp.int32)[None, :] - samples // 2
    phase = jnp.mod(row_index[:, None] * sample_index, image_rows).astype(jnp.float32) * (2.0 * math.pi / image_rows)
    scale = 1.0 / math.sqrt(samples)
    return jnp.concatenate([jnp.cos(phase) * scale, jnp.sin(phase) * scale], axis=0).astype(jnp.bfloat16)

def apply_phase(mixed, offset, sample_index, samples, image_rows, width):
    angle = jnp.mod(offset * (sample_index - samples // 2), image_rows).astype(jnp.float32) * (2.0 * math.pi / image_rows)
    cosine = jnp.cos(angle)[:, None]
    sine = jnp.sin(angle)[:, None]
    real_part = mixed[:, :width]
    imag_part = mixed[:, width:]
    return jnp.concatenate([real_part * cosine - imag_part * sine, real_part * sine + imag_part * cosine], axis=1).astype(jnp.bfloat16)

def reference(spectra, offsets):
    columns = column_table(KA, COLS)
    table = row_table(jnp.arange(ROWS, dtype=jnp.int32), KR, ROWS)
    samples_all = jnp.arange(KR, dtype=jnp.int32)

    def single(inputs):
        spectrum, offset = inputs
        mixed = jnp.dot(spectrum, columns, preferred_element_type=jnp.float32)
        shifted = apply_phase(mixed, offset, samples_all, KR, ROWS, COLS)
        product = jnp.dot(table, shifted, preferred_element_type=jnp.float32)
        real_part = product[:ROWS, :COLS] - product[ROWS:, COLS:]
        imag_part = product[:ROWS, COLS:] + product[ROWS:, :COLS]
        return jnp.concatenate([real_part, imag_part], axis=1)
    images = lax.map(single, (spectra, offsets))
    frames = images
    for lead in range(1, WIN):
        frames = frames + jnp.roll(images, -lead, axis=0)
    real_part = frames[:, :, :COLS]
    imag_part = frames[:, :, COLS:]
    log_power = jnp.log(1.0 + real_part * real_part + imag_part * imag_part)
    padded = jnp.pad(log_power, ((0, 0), (1, 1), (1, 1)))
    total = jnp.zeros_like(log_power)
    for row_step in range(3):
        for col_step in range(3):
            total = total + padded[:, row_step:row_step + ROWS, col_step:col_step + COLS]
    filtered = total / 9.0
    background = jnp.zeros_like(filtered)
    for behind in range(BG):
        background = background + jnp.roll(filtered, behind, axis=0)
    background = background / BG
    return jnp.transpose(filtered - background, (1, 2, 0))
```

```python
import math

import jax
import jax.numpy as jnp
import numpy as np
import ml_dtypes
from jax import lax
from jax.experimental import pallas as pl
from jax.experimental.pallas import tpu as pltpu
from jax.sharding import Mesh, PartitionSpec as P

KR = 256
KA = 1024
ROWS = 1024
COLS = 256
WIN = 8
BG = 16
SUBAP = 128
SUBS = 64
STRIPS = 8
OWN_S = SUBAP // SUBS
OWN_K = KR // STRIPS
OWN_C = COLS // SUBS
OWN_R = ROWS // STRIPS
EXT_C = OWN_C + 2
EXT_R = OWN_R + 8
LANES = 128
HALF = 64


def column_matrix():
    n = np.arange(KA)[None, :]
    col = (np.arange(SUBS)[None, :] * OWN_C + np.arange(OWN_C)[:, None]).reshape(-1, 1)
    phase = ((n * col) % KA).astype(np.float64) * (2.0 * math.pi / KA)
    scale = 1.0 / math.sqrt(KA)
    return np.concatenate([np.cos(phase) * scale, -np.sin(phase) * scale], axis=1).astype(ml_dtypes.bfloat16)


def row_matrices():
    scale = 1.0 / math.sqrt(KR)
    k = np.arange(KR)[None, :] - KR // 2
    out = np.zeros((STRIPS, 2, EXT_R, STRIPS, 2, OWN_K), np.float64)
    for strip in range(STRIPS):
        m = strip * OWN_R - 1 + np.arange(OWN_R + 2)
        valid = ((m >= 0) & (m < ROWS)).astype(np.float64)[:, None]
        phase = ((m[:, None] * k) % ROWS).astype(np.float64) * (2.0 * math.pi / ROWS)
        cosine = (np.cos(phase) * scale * valid).reshape(-1, STRIPS, OWN_K)
        sine = (np.sin(phase) * scale * valid).reshape(-1, STRIPS, OWN_K)
        n = OWN_R + 2
        out[strip, 0, :n, :, 0] = cosine
        out[strip, 0, :n, :, 1] = -sine
        out[strip, 1, :n, :, 0] = sine
        out[strip, 1, :n, :, 1] = cosine
    return out.reshape(STRIPS, 2 * EXT_R, 2 * KR).astype(ml_dtypes.bfloat16)


def window_matrix():
    frame = np.arange(SUBAP)[:, None]
    sub = (np.arange(SUBS)[None, :] * OWN_S + np.arange(OWN_S)[:, None]).reshape(1, -1)
    return (((sub - frame) % SUBAP) < WIN).astype(ml_dtypes.bfloat16)


def columns_kernel(strip_ref, offsets_ref, spectra_ref, table_ref, out_ref):
    parts = []
    for swapped in (False, True):
        for s in range(OWN_S):
            re = spectra_ref[s, :, :KA]
            im = spectra_ref[s, :, KA:]
            upper = jnp.concatenate([re, -im], axis=1)
            if swapped:
                parts += [jnp.concatenate([-im, -re], axis=1), upper]
            else:
                parts += [upper, jnp.concatenate([im, re], axis=1)]
    stack = jnp.concatenate(parts, axis=0)
    mixed = lax.dot_general(table_ref[...], stack, (((1,), (1,)), ((), ())), preferred_element_type=jnp.float32)
    lane = lax.broadcasted_iota(jnp.int32, (8, LANES), 1)
    sample = (lane & (OWN_K - 1)) + strip_ref[0] * OWN_K - KR // 2
    offset = jnp.where(lane < HALF, offsets_ref[0], offsets_ref[1])
    angle = ((offset * sample) & (ROWS - 1)).astype(jnp.float32) * (2.0 * math.pi / ROWS)
    cosine = jnp.cos(angle)[:1]
    sine = jnp.sin(angle)[:1]
    own = []
    for c in range(OWN_C):
        block = mixed[c * SUBS : (c + 1) * SUBS]
        own.append(block[:, :LANES] * cosine + block[:, LANES:] * sine)
    zero = jnp.zeros((1, LANES), jnp.float32)
    before = jnp.concatenate([zero, own[-1][: SUBS - 1]], axis=0)
    after = jnp.concatenate([own[0][1:], zero], axis=0)
    ext = [before] + own + [after]
    first = lax.broadcasted_iota(jnp.int32, (SUBS, LANES), 1) < HALF
    for j in range(EXT_C // 2):
        a, b = ext[2 * j], ext[2 * j + 1]
        for p, slab in ((0, jnp.where(first, a, pltpu.roll(b, HALF, 1))), (1, jnp.where(first, pltpu.roll(a, HALF, 1), b))):
            slab = slab.astype(jnp.bfloat16)
            at = (p * (EXT_C // 2) + j) * LANES
            for half in range(2):
                out_ref[half * SUBS : (half + 1) * SUBS, at : at + LANES] = slab


def image_kernel(data_ref, table_ref, window_ref, out_ref):
    pairs = EXT_C // 2
    width = pairs * LANES
    window = window_ref[...]
    summed = []
    for st in range(STRIPS):
        block = data_ref[st * SUBS : (st + 1) * SUBS, :]
        both = jnp.concatenate([block[:, :width], block[:, width:]], axis=0)
        summed.append(jnp.dot(window, both, preferred_element_type=jnp.float32))
    first = lax.broadcasted_iota(jnp.int32, (SUBAP, LANES), 1) < HALF
    logs = []
    for c in range(EXT_C):
        at = (c // 2) * LANES
        lanes = []
        for st in range(0, STRIPS, 2):
            a = summed[st][:, at : at + LANES]
            b = summed[st + 1][:, at : at + LANES]
            if c % 2 == 0:
                both = jnp.where(first, a, pltpu.roll(b, HALF, 1))
            else:
                both = jnp.where(first, pltpu.roll(a, HALF, 1), b)
            lanes.append(both.astype(jnp.bfloat16))
        frames = lax.dot_general(
            table_ref[...],
            jnp.concatenate(lanes, axis=1),
            (((1,), (1,)), ((), ())),
            preferred_element_type=jnp.float32,
        )
        re, im = frames[:EXT_R], frames[EXT_R:]
        logs.append(jnp.log(1.0 + re * re + im * im))
    for c in range(OWN_C):
        column = logs[c] + logs[c + 1] + logs[c + 2]
        total = column[:OWN_R] + column[1 : OWN_R + 1] + column[2 : OWN_R + 2]
        filtered = total * (1.0 / 9.0)
        back = filtered
        for step in (1, 2, 4, 8):
            back = back + pltpu.roll(back, step, 1)
        out_ref[:, c, :] = filtered - back * (1.0 / BG)


def body(spectra, offsets):
    strip = lax.axis_index("x") * 2 + lax.axis_index("zh")
    rows = lax.dynamic_index_in_dim(jnp.asarray(row_matrices()), strip, 0, keepdims=False)
    vmem = pl.BlockSpec(memory_space=pltpu.VMEM)
    smem = pl.BlockSpec(memory_space=pltpu.SMEM)
    sent = pl.pallas_call(
        columns_kernel,
        out_shape=jax.ShapeDtypeStruct((2 * SUBS, EXT_C * LANES), jnp.bfloat16),
        in_specs=[smem, smem, vmem, vmem],
        out_specs=vmem,
    )(strip.reshape(1), offsets, spectra, jnp.asarray(column_matrix()))
    sent = sent.reshape(2 * SUBS, 2, EXT_C * HALF)
    got = lax.all_to_all(sent, ("zh", "sub"), 0, 0, tiled=True)
    got = got.reshape(2 * SUBS, EXT_C * LANES)
    data = lax.all_gather(got, "x", axis=0, tiled=True)
    return pl.pallas_call(
        image_kernel,
        out_shape=jax.ShapeDtypeStruct((OWN_R, OWN_C, SUBAP), jnp.float32),
        in_specs=[vmem, vmem, vmem],
        out_specs=vmem,
    )(data, rows, jnp.asarray(window_matrix()))


def solution(mesh):
    grid = Mesh(mesh.devices.reshape(SUBS, STRIPS // 2, 2), ("sub", "x", "zh"))
    in_specs = (P("sub", ("x", "zh"), None), P("sub"))
    out_specs = P(("x", "zh"), "sub", None)
    return jax.shard_map(body, mesh=grid, in_specs=in_specs, out_specs=out_specs, check_vma=False)
```

```python
import math

import jax
import jax.numpy as jnp
import numpy as np
import ml_dtypes
from jax import lax
from jax.experimental import pallas as pl
from jax.experimental.pallas import tpu as pltpu
from jax.sharding import Mesh, PartitionSpec as P

KR = 256
KA = 1024
ROWS = 1024
COLS = 256
WIN = 8
BG = 16
SUBAP = 128
SUBS = 64
STRIPS = 8
OWN_S = SUBAP // SUBS
OWN_K = KR // STRIPS
OWN_C = COLS // SUBS
OWN_R = ROWS // STRIPS
EXT_C = OWN_C + 2
EXT_R = OWN_R + 8
LANES = 128
HALF = 64
ZL, YC, XS, ZH = 8, 8, 4, 2
BLOCK = COLS // ZL
PAIRS = BLOCK // 2 + 1
PAD_PAIRS = 20
CHUNK = OWN_S * PAD_PAIRS
TILE = OWN_S * ZL


def column_matrix():
    n = np.arange(KA)[None, :]
    pair = np.arange(PAD_PAIRS)[None, None, :]
    slot = 2 * pair + np.arange(2)[:, None, None]
    col = (np.arange(ZL)[None, :, None] * BLOCK - 1 + slot).reshape(-1, 1)
    valid = np.broadcast_to(slot < BLOCK + 2, (2, ZL, PAD_PAIRS)).reshape(-1, 1) & (col >= 0) & (col < COLS)
    phase = ((n * col) % KA).astype(np.float64) * (2.0 * math.pi / KA)
    scale = valid / math.sqrt(KA)
    return np.concatenate([np.cos(phase) * scale, -np.sin(phase) * scale], axis=1).astype(ml_dtypes.bfloat16)


def row_matrices():
    scale = 1.0 / math.sqrt(KR)
    k = np.arange(KR)[None, :] - KR // 2
    out = np.zeros((STRIPS, 2, EXT_R, STRIPS, 2, OWN_K), np.float64)
    for strip in range(STRIPS):
        m = strip * OWN_R - 1 + np.arange(OWN_R + 2)
        valid = ((m >= 0) & (m < ROWS)).astype(np.float64)[:, None]
        phase = ((m[:, None] * k) % ROWS).astype(np.float64) * (2.0 * math.pi / ROWS)
        cosine = (np.cos(phase) * scale * valid).reshape(-1, STRIPS, OWN_K)
        sine = (np.sin(phase) * scale * valid).reshape(-1, STRIPS, OWN_K)
        n = OWN_R + 2
        out[strip, 0, :n, :, 0] = cosine
        out[strip, 0, :n, :, 1] = -sine
        out[strip, 1, :n, :, 0] = sine
        out[strip, 1, :n, :, 1] = cosine
    return out.reshape(STRIPS, 2 * EXT_R, 2 * KR).astype(ml_dtypes.bfloat16)


def window_matrix():
    frame = np.arange(SUBAP)[:, None]
    yc, p, z = np.meshgrid(np.arange(YC), np.arange(OWN_S), np.arange(ZL), indexing="ij")
    sub = (OWN_S * (z * YC + yc) + p).reshape(1, -1)
    return (((sub - frame) % SUBAP) < WIN).astype(ml_dtypes.bfloat16)


def order_matrix():
    pair, p, z = np.meshgrid(np.arange(PAIRS), np.arange(OWN_S), np.arange(ZL), indexing="ij")
    source = (z * OWN_S + p) * PAD_PAIRS + pair
    return (source.reshape(-1, 1) == np.arange(ZL * CHUNK)[None, :]).astype(ml_dtypes.bfloat16)


def columns_kernel(strip_ref, offsets_ref, spectra_ref, table_ref, out_ref):
    parts = []
    for swapped in (False, True):
        for s in range(OWN_S):
            re = spectra_ref[s, :, :KA]
            im = spectra_ref[s, :, KA:]
            upper = jnp.concatenate([re, -im], axis=1)
            if swapped:
                parts += [jnp.concatenate([-im, -re], axis=1), upper]
            else:
                parts += [upper, jnp.concatenate([im, re], axis=1)]
    stack = jnp.concatenate(parts, axis=0)
    mixed = lax.dot_general(table_ref[...], stack, (((1,), (1,)), ((), ())), preferred_element_type=jnp.float32)
    lane = lax.broadcasted_iota(jnp.int32, (8, LANES), 1)
    sample = (lane & (OWN_K - 1)) + strip_ref[0] * OWN_K - KR // 2
    offset = jnp.where(lane < HALF, offsets_ref[0], offsets_ref[1])
    angle = ((offset * sample) & (ROWS - 1)).astype(jnp.float32) * (2.0 * math.pi / ROWS)
    cosine = jnp.cos(angle)[:1]
    sine = jnp.sin(angle)[:1]
    shifted = mixed[:, :LANES] * cosine + mixed[:, LANES:] * sine
    rows = ZL * PAD_PAIRS
    even, odd = shifted[:rows], shifted[rows:]
    first = lax.broadcasted_iota(jnp.int32, (rows, LANES), 1) < HALF
    slabs = (jnp.where(first, even, pltpu.roll(odd, HALF, 1)), jnp.where(first, pltpu.roll(even, HALF, 1), odd))
    for z in range(ZL):
        block = jnp.concatenate([slab[z * PAD_PAIRS : (z + 1) * PAD_PAIRS] for slab in slabs], axis=0).astype(jnp.bfloat16)
        for half in range(ZH):
            out_ref[half * ZL + z] = block


def order_kernel(data_ref, order_ref, out_ref):
    both = jnp.concatenate([data_ref[h * ZL : (h + 1) * ZL].reshape(ZL * CHUNK, LANES) for h in range(ZH)], axis=1)
    rows = jnp.dot(order_ref[...], both, preferred_element_type=jnp.float32).astype(jnp.bfloat16)
    for j in range(YC):
        for t in range(EXT_C // 2):
            for h in range(ZH):
                tile = rows[(2 * j + t) * TILE : (2 * j + t + 1) * TILE, h * LANES : (h + 1) * LANES]
                for x in range(XS):
                    out_ref[x * YC + j, (t * ZH + h) * TILE : (t * ZH + h + 1) * TILE, :] = tile


def image_kernel(data_ref, table_ref, window_ref, out_ref):
    window = window_ref[...]
    summed = []
    for x in range(XS):
        for h in range(ZH):
            slabs = []
            for t in range(EXT_C // 2):
                at = (t * ZH + h) * TILE
                slabs.append(jnp.concatenate([data_ref[x * YC + j, at : at + TILE, :] for j in range(YC)], axis=0))
            summed.append(jnp.dot(window, jnp.concatenate(slabs, axis=1), preferred_element_type=jnp.float32))
    first = lax.broadcasted_iota(jnp.int32, (SUBAP, LANES), 1) < HALF
    logs = []
    for c in range(EXT_C):
        at = (c // 2) * LANES
        lanes = []
        for st in range(0, STRIPS, 2):
            a = summed[st][:, at : at + LANES]
            b = summed[st + 1][:, at : at + LANES]
            if c % 2 == 0:
                both = jnp.where(first, a, pltpu.roll(b, HALF, 1))
            else:
                both = jnp.where(first, pltpu.roll(a, HALF, 1), b)
            lanes.append(both.astype(jnp.bfloat16))
        frames = lax.dot_general(
            table_ref[...],
            jnp.concatenate(lanes, axis=1),
            (((1,), (1,)), ((), ())),
            preferred_element_type=jnp.float32,
        )
        re, im = frames[:EXT_R], frames[EXT_R:]
        logs.append(jnp.log(1.0 + re * re + im * im))
    for c in range(OWN_C):
        column = logs[c] + logs[c + 1] + logs[c + 2]
        total = column[:OWN_R] + column[1 : OWN_R + 1] + column[2 : OWN_R + 2]
        filtered = total * (1.0 / 9.0)
        back = filtered
        for step in (1, 2, 4, 8):
            back = back + pltpu.roll(back, step, 1)
        out_ref[:, c, :] = filtered - back * (1.0 / BG)


def body(spectra, offsets):
    strip = lax.axis_index("x") * ZH + lax.axis_index("zh")
    rows = lax.dynamic_index_in_dim(jnp.asarray(row_matrices()), strip, 0, keepdims=False)
    vmem = pl.BlockSpec(memory_space=pltpu.VMEM)
    smem = pl.BlockSpec(memory_space=pltpu.SMEM)
    sent = pl.pallas_call(
        columns_kernel,
        out_shape=jax.ShapeDtypeStruct((ZH * ZL, CHUNK, LANES), jnp.bfloat16),
        in_specs=[smem, smem, vmem, vmem],
        out_specs=vmem,
    )(strip.reshape(1), offsets, spectra, jnp.asarray(column_matrix()))
    got = lax.all_to_all(sent, ("zh", "zl"), 0, 0, tiled=True)
    sent = pl.pallas_call(
        order_kernel,
        out_shape=jax.ShapeDtypeStruct((XS * YC, EXT_C // 2 * ZH * TILE, LANES), jnp.bfloat16),
        in_specs=[vmem, vmem],
        out_specs=vmem,
    )(got, jnp.asarray(order_matrix()))
    data = lax.all_to_all(sent, ("x", "y", "co"), 0, 0, tiled=True)
    return pl.pallas_call(
        image_kernel,
        out_shape=jax.ShapeDtypeStruct((OWN_R, OWN_C, SUBAP), jnp.float32),
        in_specs=[vmem, vmem, vmem],
        out_specs=vmem,
    )(data, rows, jnp.asarray(window_matrix()))


def solution(mesh):
    grid = Mesh(mesh.devices.reshape(ZL, YC // 2, 2, XS, ZH), ("zl", "y", "co", "x", "zh"))
    in_specs = (P(("zl", "y", "co"), ("x", "zh"), None), P(("zl", "y", "co")))
    out_specs = P(("x", "zh"), ("zl", "y", "co"), None)
    return jax.shard_map(body, mesh=grid, in_specs=in_specs, out_specs=out_specs, check_vma=False)
```

```python
import math

import jax
import jax.numpy as jnp
import numpy as np
import ml_dtypes
from jax import lax
from jax.experimental import pallas as pl
from jax.experimental.pallas import tpu as pltpu
from jax.sharding import Mesh, PartitionSpec as P

KR = 256
KA = 1024
ROWS = 1024
COLS = 256
WIN = 8
BG = 16
SUBAP = 128
SUBS = 64
STRIPS = 8
OWN_S = SUBAP // SUBS
OWN_K = KR // STRIPS
OWN_C = COLS // SUBS
OWN_R = ROWS // STRIPS
EXT_C = OWN_C + 2
EXT_R = OWN_R + 8
VMEM_BYTES = 24 << 20
LANES = 128
HALF = 64
ZL, YC, XS, ZH = 8, 8, 4, 2
BLOCK = COLS // ZL
PAIRS = BLOCK // 2 + 1
PAD_PAIRS = 20
CHUNK = OWN_S * PAD_PAIRS
TILE = OWN_S * ZL


def column_matrix():
    n = np.arange(KA)[None, :]
    pair = np.arange(PAD_PAIRS)[None, None, :]
    slot = 2 * pair + np.arange(2)[:, None, None]
    col = (np.arange(ZL)[None, :, None] * BLOCK - 1 + slot).reshape(-1, 1)
    valid = np.broadcast_to(slot < BLOCK + 2, (2, ZL, PAD_PAIRS)).reshape(-1, 1) & (col >= 0) & (col < COLS)
    phase = ((n * col) % KA).astype(np.float64) * (2.0 * math.pi / KA)
    scale = valid / math.sqrt(KA)
    return np.concatenate([np.cos(phase) * scale, -np.sin(phase) * scale], axis=1).astype(ml_dtypes.bfloat16)


def row_matrices():
    scale = 1.0 / math.sqrt(KR)
    k = np.arange(KR)[None, :] - KR // 2
    out = np.zeros((STRIPS, 2, EXT_R, STRIPS, 2, OWN_K), np.float64)
    for strip in range(STRIPS):
        m = strip * OWN_R - 1 + np.arange(OWN_R + 2)
        valid = ((m >= 0) & (m < ROWS)).astype(np.float64)[:, None]
        phase = ((m[:, None] * k) % ROWS).astype(np.float64) * (2.0 * math.pi / ROWS)
        cosine = (np.cos(phase) * scale * valid).reshape(-1, STRIPS, OWN_K)
        sine = (np.sin(phase) * scale * valid).reshape(-1, STRIPS, OWN_K)
        n = OWN_R + 2
        out[strip, 0, :n, :, 0] = cosine
        out[strip, 0, :n, :, 1] = -sine
        out[strip, 1, :n, :, 0] = sine
        out[strip, 1, :n, :, 1] = cosine
    return out.reshape(STRIPS, 2 * EXT_R, 2 * KR).astype(ml_dtypes.bfloat16)


def window_matrix():
    frame = lax.broadcasted_iota(jnp.int32, (SUBAP, SUBAP), 0)
    lane = lax.broadcasted_iota(jnp.int32, (SUBAP, SUBAP), 1)
    sub = OWN_S * ((lane & (ZL - 1)) * YC + (lane >> 4)) + ((lane >> 3) & 1)
    return jnp.where(((sub - frame) & (SUBAP - 1)) < WIN, 1.0, 0.0).astype(jnp.bfloat16)


def order_matrix():
    row = lax.broadcasted_iota(jnp.int32, (PAIRS * TILE, ZL * CHUNK), 0)
    lane = lax.broadcasted_iota(jnp.int32, (PAIRS * TILE, ZL * CHUNK), 1)
    source = ((row & (ZL - 1)) * OWN_S + ((row >> 3) & 1)) * PAD_PAIRS + (row >> 4)
    return jnp.where(source == lane, 1.0, 0.0).astype(jnp.bfloat16)


def columns_kernel(strip_ref, offsets_hbm, spectra_hbm, table_hbm, out_ref, offsets_ref, spectra_ref, table_ref, arrived):
    rows = ZL * PAD_PAIRS
    fetches = [pltpu.make_async_copy(spectra_hbm, spectra_ref, arrived.at[0])]
    for i in range(2):
        part = pl.ds(i * rows, rows)
        fetches.append(pltpu.make_async_copy(table_hbm.at[part], table_ref.at[part], arrived.at[i + 1]))
    small = pltpu.make_async_copy(offsets_hbm, offsets_ref, arrived.at[3])
    for fetch in [small] + fetches:
        fetch.start()
    small.wait()
    lane = lax.broadcasted_iota(jnp.int32, (8, LANES), 1)
    sample = (lane & (OWN_K - 1)) + strip_ref[0] * OWN_K - KR // 2
    offset = jnp.where(lane < HALF, offsets_ref[0], offsets_ref[1])
    angle = ((offset * sample) & (ROWS - 1)).astype(jnp.float32) * (2.0 * math.pi / ROWS)
    cosine = jnp.cos(angle)[:1]
    sine = jnp.sin(angle)[:1]
    fetches[0].wait()
    parts = []
    for swapped in (False, True):
        for s in range(OWN_S):
            re = spectra_ref[s, :, :KA]
            im = spectra_ref[s, :, KA:]
            upper = jnp.concatenate([re, -im], axis=1)
            if swapped:
                parts += [jnp.concatenate([-im, -re], axis=1), upper]
            else:
                parts += [upper, jnp.concatenate([im, re], axis=1)]
    stack = jnp.concatenate(parts, axis=0)
    shifted = []
    for i in range(2):
        fetches[i + 1].wait()
        mixed = lax.dot_general(
            table_ref[i * rows : (i + 1) * rows], stack, (((1,), (1,)), ((), ())), preferred_element_type=jnp.float32
        )
        shifted.append(mixed[:, :LANES] * cosine + mixed[:, LANES:] * sine)
    even, odd = shifted
    first = lax.broadcasted_iota(jnp.int32, (rows, LANES), 1) < HALF
    slabs = (jnp.where(first, even, pltpu.roll(odd, HALF, 1)), jnp.where(first, pltpu.roll(even, HALF, 1), odd))
    for z in range(ZL):
        block = jnp.concatenate([slab[z * PAD_PAIRS : (z + 1) * PAD_PAIRS] for slab in slabs], axis=0).astype(jnp.bfloat16)
        for half in range(ZH):
            out_ref[half * ZL + z] = block


def order_kernel(data_ref, out_ref):
    both = jnp.concatenate([data_ref[h * ZL : (h + 1) * ZL].reshape(ZL * CHUNK, LANES) for h in range(ZH)], axis=1)
    rows = jnp.dot(order_matrix(), both, preferred_element_type=jnp.float32).astype(jnp.bfloat16)
    for j in range(YC):
        for t in range(EXT_C // 2):
            for h in range(ZH):
                tile = rows[(2 * j + t) * TILE : (2 * j + t + 1) * TILE, h * LANES : (h + 1) * LANES]
                for x in range(XS):
                    out_ref[x * YC + j, (t * ZH + h) * TILE : (t * ZH + h + 1) * TILE, :] = tile


def image_kernel(strip_ref, data_ref, tables_ref, out_ref, table_ref, arrived):
    fetch = pltpu.make_async_copy(tables_ref.at[strip_ref[0]], table_ref, arrived)
    fetch.start()
    window = window_matrix()
    summed = []
    for x in range(XS):
        for h in range(ZH):
            slabs = []
            for t in range(EXT_C // 2):
                at = (t * ZH + h) * TILE
                slabs.append(jnp.concatenate([data_ref[x * YC + j, at : at + TILE, :] for j in range(YC)], axis=0))
            summed.append(jnp.dot(window, jnp.concatenate(slabs, axis=1), preferred_element_type=jnp.float32))
    first = lax.broadcasted_iota(jnp.int32, (SUBAP, LANES), 1) < HALF
    fetch.wait()
    logs = []
    for c in range(EXT_C):
        at = (c // 2) * LANES
        lanes = []
        for st in range(0, STRIPS, 2):
            a = summed[st][:, at : at + LANES]
            b = summed[st + 1][:, at : at + LANES]
            if c % 2 == 0:
                both = jnp.where(first, a, pltpu.roll(b, HALF, 1))
            else:
                both = jnp.where(first, pltpu.roll(a, HALF, 1), b)
            lanes.append(both.astype(jnp.bfloat16))
        frames = lax.dot_general(
            table_ref[...],
            jnp.concatenate(lanes, axis=1),
            (((1,), (1,)), ((), ())),
            preferred_element_type=jnp.float32,
        )
        re, im = frames[:EXT_R], frames[EXT_R:]
        logs.append(jnp.log(1.0 + re * re + im * im))
    for c in range(OWN_C):
        column = logs[c] + logs[c + 1] + logs[c + 2]
        total = column[:OWN_R] + column[1 : OWN_R + 1] + column[2 : OWN_R + 2]
        filtered = total * (1.0 / 9.0)
        back = filtered
        for step in (1, 2, 4, 8):
            back = back + pltpu.roll(back, step, 1)
        out_ref[:, c, :] = filtered - back * (1.0 / BG)


def body(spectra, offsets):
    strip = (lax.axis_index("x") * ZH + lax.axis_index("zh")).reshape(1)
    vmem = pl.BlockSpec(memory_space=pltpu.VMEM)
    smem = pl.BlockSpec(memory_space=pltpu.SMEM)
    hbm = pl.BlockSpec(memory_space=pltpu.HBM)
    params = pltpu.CompilerParams(vmem_limit_bytes=VMEM_BYTES)
    columns = jnp.asarray(column_matrix())
    sent = pl.pallas_call(
        columns_kernel,
        out_shape=jax.ShapeDtypeStruct((ZH * ZL, CHUNK, LANES), jnp.bfloat16),
        in_specs=[smem, hbm, hbm, hbm],
        out_specs=vmem,
        scratch_shapes=[
            pltpu.SMEM(offsets.shape, jnp.int32),
            pltpu.VMEM(spectra.shape, jnp.bfloat16),
            pltpu.VMEM(columns.shape, jnp.bfloat16),
            pltpu.SemaphoreType.DMA((4,)),
        ],
        compiler_params=params,
    )(
        strip,
        pltpu.with_memory_space_constraint(offsets, pltpu.HBM),
        pltpu.with_memory_space_constraint(spectra, pltpu.HBM),
        pltpu.with_memory_space_constraint(columns, pltpu.HBM),
    )
    got = lax.all_to_all(sent, ("zh", "zl"), 0, 0, tiled=True)
    sent = pl.pallas_call(
        order_kernel,
        out_shape=jax.ShapeDtypeStruct((XS * YC, EXT_C // 2 * ZH * TILE, LANES), jnp.bfloat16),
        in_specs=[vmem],
        out_specs=vmem,
        compiler_params=params,
    )(got)
    data = lax.all_to_all(sent, ("x", "y", "co"), 0, 0, tiled=True)
    return pl.pallas_call(
        image_kernel,
        out_shape=jax.ShapeDtypeStruct((OWN_R, OWN_C, SUBAP), jnp.float32),
        in_specs=[smem, vmem, hbm],
        out_specs=vmem,
        scratch_shapes=[pltpu.VMEM((2 * EXT_R, 2 * KR), jnp.bfloat16), pltpu.SemaphoreType.DMA],
        compiler_params=params,
    )(strip, data, pltpu.with_memory_space_constraint(jnp.asarray(row_matrices()), pltpu.HBM))


def solution(mesh):
    grid = Mesh(mesh.devices.reshape(ZL, YC // 2, 2, XS, ZH), ("zl", "y", "co", "x", "zh"))
    in_specs = (P(("zl", "y", "co"), ("x", "zh"), None), P(("zl", "y", "co")))
    out_specs = P(("x", "zh"), ("zl", "y", "co"), None)
    return jax.shard_map(body, mesh=grid, in_specs=in_specs, out_specs=out_specs, check_vma=False)
```

```python
import math

import jax
import jax.numpy as jnp
import numpy as np
import ml_dtypes
from jax import lax
from jax.experimental import pallas as pl
from jax.experimental.pallas import tpu as pltpu
from jax.sharding import Mesh, PartitionSpec as P

KR = 256
KA = 1024
ROWS = 1024
COLS = 256
WIN = 8
BG = 16
SUBAP = 128
SUBS = 64
STRIPS = 8
OWN_S = SUBAP // SUBS
OWN_K = KR // STRIPS
OWN_C = COLS // SUBS
OWN_R = ROWS // STRIPS
EXT_C = OWN_C + 2
EXT_R = OWN_R + 8
VMEM_BYTES = 24 << 20
LANES = 128
HALF = 64
ZL, YC, XS, ZH = 8, 8, 4, 2
BLOCK = COLS // ZL
PAIRS = BLOCK // 2 + 1
SLOTS = BLOCK + 4
TILE = OWN_S * ZL


def column_matrix():
    n = np.arange(KA)[None, :]
    slot = np.arange(SLOTS)[None, :]
    col = (np.arange(ZL)[:, None] * BLOCK - 1 + slot).reshape(-1, 1)
    valid = np.broadcast_to(slot < BLOCK + 2, (ZL, SLOTS)).reshape(-1, 1) & (col >= 0) & (col < COLS)
    phase = ((n * col) % KA).astype(np.float64) * (2.0 * math.pi / KA)
    scale = valid / math.sqrt(KA)
    return np.concatenate([np.cos(phase) * scale, -np.sin(phase) * scale], axis=1).astype(ml_dtypes.bfloat16)


def row_matrices():
    scale = 1.0 / math.sqrt(KR)
    k = np.arange(KR)[None, :] - KR // 2
    out = np.zeros((STRIPS, 2, EXT_R, STRIPS, 2, OWN_K), np.float64)
    for strip in range(STRIPS):
        m = strip * OWN_R - 1 + np.arange(OWN_R + 2)
        valid = ((m >= 0) & (m < ROWS)).astype(np.float64)[:, None]
        phase = ((m[:, None] * k) % ROWS).astype(np.float64) * (2.0 * math.pi / ROWS)
        cosine = (np.cos(phase) * scale * valid).reshape(-1, STRIPS, OWN_K)
        sine = (np.sin(phase) * scale * valid).reshape(-1, STRIPS, OWN_K)
        n = OWN_R + 2
        out[strip, 0, :n, :, 0] = cosine
        out[strip, 0, :n, :, 1] = -sine
        out[strip, 1, :n, :, 0] = sine
        out[strip, 1, :n, :, 1] = cosine
    return out.reshape(STRIPS, 2 * EXT_R, 2 * KR).astype(ml_dtypes.bfloat16)


def window_matrix():
    frame = lax.broadcasted_iota(jnp.int32, (SUBAP, SUBAP), 0)
    lane = lax.broadcasted_iota(jnp.int32, (SUBAP, SUBAP), 1)
    sub = OWN_S * ((lane & (ZL - 1)) * YC + (lane >> 4)) + ((lane >> 3) & 1)
    return jnp.where(((sub - frame) & (SUBAP - 1)) < WIN, 1.0, 0.0).astype(jnp.bfloat16)


def order_matrix():
    row = lax.broadcasted_iota(jnp.int32, (PAIRS * TILE, ZL * SLOTS), 0)
    lane = lax.broadcasted_iota(jnp.int32, (PAIRS * TILE, ZL * SLOTS), 1)
    source = (row & (ZL - 1)) * SLOTS + (row >> 3)
    return jnp.where(source == lane, 1.0, 0.0).astype(jnp.bfloat16)


def columns_kernel(strip_ref, offsets_hbm, spectra_hbm, table_hbm, out_ref, offsets_ref, spectra_ref, table_ref, arrived):
    rows = ZL * SLOTS // 2
    fetches = [pltpu.make_async_copy(spectra_hbm, spectra_ref, arrived.at[0])]
    for i in range(2):
        part = pl.ds(i * rows, rows)
        fetches.append(pltpu.make_async_copy(table_hbm.at[part], table_ref.at[part], arrived.at[i + 1]))
    small = pltpu.make_async_copy(offsets_hbm, offsets_ref, arrived.at[3])
    for fetch in [small] + fetches:
        fetch.start()
    small.wait()
    lane = lax.broadcasted_iota(jnp.int32, (8, LANES), 1)
    sample = (lane & (OWN_K - 1)) + strip_ref[0] * OWN_K - KR // 2
    offset = jnp.where(lane < HALF, offsets_ref[0], offsets_ref[1])
    angle = ((offset * sample) & (ROWS - 1)).astype(jnp.float32) * (2.0 * math.pi / ROWS)
    cosine = jnp.cos(angle)[:1]
    sine = jnp.sin(angle)[:1]
    fetches[0].wait()
    parts = []
    for swapped in (False, True):
        for s in range(OWN_S):
            re = spectra_ref[s, :, :KA]
            im = spectra_ref[s, :, KA:]
            upper = jnp.concatenate([re, -im], axis=1)
            if swapped:
                parts += [jnp.concatenate([-im, -re], axis=1), upper]
            else:
                parts += [upper, jnp.concatenate([im, re], axis=1)]
    stack = jnp.concatenate(parts, axis=0)
    shifted = []
    for i in range(2):
        fetches[i + 1].wait()
        mixed = lax.dot_general(
            table_ref[i * rows : (i + 1) * rows], stack, (((1,), (1,)), ((), ())), preferred_element_type=jnp.float32
        )
        shifted.append(mixed[:, :LANES] * cosine + mixed[:, LANES:] * sine)
    shifted = jnp.concatenate(shifted, axis=0)
    turned = pltpu.roll(shifted, HALF, 1)
    odd_row = lax.broadcasted_iota(jnp.int32, shifted.shape, 0) & 1
    last = lax.broadcasted_iota(jnp.int32, shifted.shape, 1) >> 6
    partner = jnp.where(odd_row == 1, pltpu.roll(turned, 1, 0), pltpu.roll(turned, 2 * rows - 1, 0))
    result = jnp.where(odd_row == last, shifted, partner).astype(jnp.bfloat16).reshape(rows, 2, LANES)
    for half in range(ZH):
        out_ref[half * rows : (half + 1) * rows] = result


def order_kernel(data_ref, out_ref):
    rows = ZL * SLOTS // 2
    both = jnp.concatenate([data_ref[h * rows : (h + 1) * rows].reshape(2 * rows, LANES) for h in range(ZH)], axis=1)
    rows = jnp.dot(order_matrix(), both, preferred_element_type=jnp.float32).astype(jnp.bfloat16)
    for j in range(YC):
        for t in range(EXT_C // 2):
            for h in range(ZH):
                tile = rows[(2 * j + t) * TILE : (2 * j + t + 1) * TILE, h * LANES : (h + 1) * LANES]
                for x in range(XS):
                    out_ref[x * YC + j, (t * ZH + h) * TILE : (t * ZH + h + 1) * TILE, :] = tile


def image_kernel(strip_ref, data_ref, tables_ref, out_ref, table_ref, arrived):
    fetch = pltpu.make_async_copy(tables_ref.at[strip_ref[0]], table_ref, arrived)
    fetch.start()
    window = window_matrix()
    summed = []
    for x in range(XS):
        for h in range(ZH):
            slabs = []
            for t in range(EXT_C // 2):
                at = (t * ZH + h) * TILE
                slabs.append(jnp.concatenate([data_ref[x * YC + j, at : at + TILE, :] for j in range(YC)], axis=0))
            summed.append(jnp.dot(window, jnp.concatenate(slabs, axis=1), preferred_element_type=jnp.float32))
    first = lax.broadcasted_iota(jnp.int32, (SUBAP, LANES), 1) < HALF
    fetch.wait()
    logs = []
    for c in range(EXT_C):
        at = (c // 2) * LANES
        lanes = []
        for st in range(0, STRIPS, 2):
            a = summed[st][:, at : at + LANES]
            b = summed[st + 1][:, at : at + LANES]
            if c % 2 == 0:
                both = jnp.where(first, a, pltpu.roll(b, HALF, 1))
            else:
                both = jnp.where(first, pltpu.roll(a, HALF, 1), b)
            lanes.append(both.astype(jnp.bfloat16))
        frames = lax.dot_general(
            table_ref[...],
            jnp.concatenate(lanes, axis=1),
            (((1,), (1,)), ((), ())),
            preferred_element_type=jnp.float32,
        )
        re, im = frames[:EXT_R], frames[EXT_R:]
        logs.append(jnp.log(1.0 + re * re + im * im))
    for c in range(OWN_C):
        column = logs[c] + logs[c + 1] + logs[c + 2]
        total = column[:OWN_R] + column[1 : OWN_R + 1] + column[2 : OWN_R + 2]
        filtered = total * (1.0 / 9.0)
        back = filtered
        for step in (1, 2, 4, 8):
            back = back + pltpu.roll(back, step, 1)
        out_ref[:, c, :] = filtered - back * (1.0 / BG)


def body(spectra, offsets):
    strip = (lax.axis_index("x") * ZH + lax.axis_index("zh")).reshape(1)
    vmem = pl.BlockSpec(memory_space=pltpu.VMEM)
    smem = pl.BlockSpec(memory_space=pltpu.SMEM)
    hbm = pl.BlockSpec(memory_space=pltpu.HBM)
    params = pltpu.CompilerParams(vmem_limit_bytes=VMEM_BYTES)
    columns = jnp.asarray(column_matrix())
    sent = pl.pallas_call(
        columns_kernel,
        out_shape=jax.ShapeDtypeStruct((ZH * ZL * SLOTS // 2, 2, LANES), jnp.bfloat16),
        in_specs=[smem, hbm, hbm, hbm],
        out_specs=vmem,
        scratch_shapes=[
            pltpu.SMEM(offsets.shape, jnp.int32),
            pltpu.VMEM(spectra.shape, jnp.bfloat16),
            pltpu.VMEM(columns.shape, jnp.bfloat16),
            pltpu.SemaphoreType.DMA((4,)),
        ],
        compiler_params=params,
    )(
        strip,
        pltpu.with_memory_space_constraint(offsets, pltpu.HBM),
        pltpu.with_memory_space_constraint(spectra, pltpu.HBM),
        pltpu.with_memory_space_constraint(columns, pltpu.HBM),
    )
    got = lax.all_to_all(sent.reshape(ZH * ZL, SLOTS // 2, 2, LANES), ("zh", "zl"), 0, 0, tiled=True)
    sent = pl.pallas_call(
        order_kernel,
        out_shape=jax.ShapeDtypeStruct((XS * YC, EXT_C // 2 * ZH * TILE, LANES), jnp.bfloat16),
        in_specs=[vmem],
        out_specs=vmem,
        compiler_params=params,
    )(got.reshape(sent.shape))
    data = lax.all_to_all(sent, ("x", "y", "co"), 0, 0, tiled=True)
    return pl.pallas_call(
        image_kernel,
        out_shape=jax.ShapeDtypeStruct((OWN_R, OWN_C, SUBAP), jnp.float32),
        in_specs=[smem, vmem, hbm],
        out_specs=vmem,
        scratch_shapes=[pltpu.VMEM((2 * EXT_R, 2 * KR), jnp.bfloat16), pltpu.SemaphoreType.DMA],
        compiler_params=params,
    )(strip, data, pltpu.with_memory_space_constraint(jnp.asarray(row_matrices()), pltpu.HBM))


def solution(mesh):
    grid = Mesh(mesh.devices.reshape(ZL, YC // 2, 2, XS, ZH), ("zl", "y", "co", "x", "zh"))
    in_specs = (P(("zl", "y", "co"), ("x", "zh"), None), P(("zl", "y", "co")))
    out_specs = P(("x", "zh"), ("zl", "y", "co"), None)
    return jax.shard_map(body, mesh=grid, in_specs=in_specs, out_specs=out_specs, check_vma=False)
```

```python
import math

import jax
import jax.numpy as jnp
import numpy as np
import ml_dtypes
from jax import lax
from jax.experimental import pallas as pl
from jax.experimental.pallas import tpu as pltpu
from jax.sharding import Mesh, PartitionSpec as P

KR = 256
KA = 1024
ROWS = 1024
COLS = 256
WIN = 8
BG = 16
SUBAP = 128
SUBS = 64
STRIPS = 8
OWN_S = SUBAP // SUBS
OWN_K = KR // STRIPS
OWN_C = COLS // SUBS
OWN_R = ROWS // STRIPS
EXT_C = OWN_C + 2
EXT_R = OWN_R + 8
VMEM_BYTES = 24 << 20
LANES = 128
HALF = 64
ZL, YC, XS, ZH = 8, 8, 4, 2
BLOCK = COLS // ZL
PAIRS = BLOCK // 2 + 1
SLOTS = BLOCK + 4
TILE = OWN_S * ZL


def column_matrix():
    n = np.arange(KA)[None, :]
    slot = np.arange(SLOTS)[None, :]
    col = (np.arange(ZL)[:, None] * BLOCK - 1 + slot).reshape(-1, 1)
    valid = np.broadcast_to(slot < BLOCK + 2, (ZL, SLOTS)).reshape(-1, 1) & (col >= 0) & (col < COLS)
    phase = ((n * col) % KA).astype(np.float64) * (2.0 * math.pi / KA)
    scale = valid / math.sqrt(KA)
    return np.stack([np.cos(phase) * scale, -np.sin(phase) * scale]).astype(ml_dtypes.bfloat16)


def row_matrices():
    scale = 1.0 / math.sqrt(KR)
    k = np.arange(KR)[None, :] - KR // 2
    out = np.zeros((STRIPS, 2, EXT_R, STRIPS, 2, OWN_K), np.float64)
    for strip in range(STRIPS):
        m = strip * OWN_R - 1 + np.arange(OWN_R + 2)
        valid = ((m >= 0) & (m < ROWS)).astype(np.float64)[:, None]
        phase = ((m[:, None] * k) % ROWS).astype(np.float64) * (2.0 * math.pi / ROWS)
        cosine = (np.cos(phase) * scale * valid).reshape(-1, STRIPS, OWN_K)
        sine = (np.sin(phase) * scale * valid).reshape(-1, STRIPS, OWN_K)
        n = OWN_R + 2
        out[strip, 0, :n, :, 0] = cosine
        out[strip, 0, :n, :, 1] = -sine
        out[strip, 1, :n, :, 0] = sine
        out[strip, 1, :n, :, 1] = cosine
    return out.reshape(STRIPS, 2 * EXT_R, 2 * KR).astype(ml_dtypes.bfloat16)


def window_matrix():
    frame = lax.broadcasted_iota(jnp.int32, (SUBAP, SUBAP), 0)
    lane = lax.broadcasted_iota(jnp.int32, (SUBAP, SUBAP), 1)
    sub = OWN_S * ((lane & (ZL - 1)) * YC + (lane >> 4)) + ((lane >> 3) & 1)
    return jnp.where(((sub - frame) & (SUBAP - 1)) < WIN, 1.0, 0.0).astype(jnp.bfloat16)


def order_matrix():
    row = lax.broadcasted_iota(jnp.int32, (PAIRS * TILE, ZL * SLOTS), 0)
    lane = lax.broadcasted_iota(jnp.int32, (PAIRS * TILE, ZL * SLOTS), 1)
    source = (row & (ZL - 1)) * SLOTS + (row >> 3)
    return jnp.where(source == lane, 1.0, 0.0).astype(jnp.bfloat16)


def columns_kernel(
    strip_ref, offsets_hbm, spectra_hbm, table_hbm, tables_hbm, out_ref, rows_ref, offsets_ref, spectra_ref, table_ref, arrived
):
    small = pltpu.make_async_copy(offsets_hbm, offsets_ref, arrived.at[0])
    whole = pltpu.make_async_copy(spectra_hbm, spectra_ref, arrived.at[1])
    rows = pltpu.make_async_copy(tables_hbm.at[strip_ref[0]], rows_ref, arrived.at[2])
    fetches = [pltpu.make_async_copy(table_hbm.at[i], table_ref.at[i], arrived.at[3 + i]) for i in range(2)]
    for fetch in [small, whole] + fetches + [rows]:
        fetch.start()
    small.wait()
    lane = lax.broadcasted_iota(jnp.int32, (8, LANES), 1)
    sample = (lane & (OWN_K - 1)) + strip_ref[0] * OWN_K - KR // 2
    offset = jnp.where(lane < HALF, offsets_ref[0], offsets_ref[1])
    angle = ((offset * sample) & (ROWS - 1)).astype(jnp.float32) * (2.0 * math.pi / ROWS)
    cosine = jnp.cos(angle)[:1]
    sine = jnp.sin(angle)
    sine = jnp.where((lane & OWN_K) == 0, -sine, sine)[:1]
    whole.wait()
    re = [spectra_ref[s, :, :KA] for s in range(OWN_S)]
    im = [spectra_ref[s, :, KA:] for s in range(OWN_S)]
    mixed = None
    for fetch, part in zip(fetches, (0, 1)):
        if part == 0:
            stack = jnp.concatenate([re[0], im[0], re[1], im[1]], axis=0)
        else:
            stack = jnp.concatenate([-im[0], re[0], -im[1], re[1]], axis=0)
        fetch.wait()
        product = lax.dot_general(table_ref[part], stack, (((1,), (1,)), ((), ())), preferred_element_type=jnp.float32)
        mixed = product if mixed is None else mixed + product
    lanes = lax.broadcasted_iota(jnp.int32, mixed.shape, 1)
    other = jnp.where((lanes & OWN_K) == 0, pltpu.roll(mixed, LANES - OWN_K, 1), pltpu.roll(mixed, OWN_K, 1))
    shifted = mixed * cosine + other * sine
    turned = pltpu.roll(shifted, HALF, 1)
    odd_row = lax.broadcasted_iota(jnp.int32, shifted.shape, 0) & 1
    partner = jnp.where(odd_row == 1, pltpu.roll(turned, 1, 0), pltpu.roll(turned, ZL * SLOTS - 1, 0))
    pairs = ZL * SLOTS // 2
    result = jnp.where(odd_row == lanes >> 6, shifted, partner).astype(jnp.bfloat16).reshape(pairs, 2, LANES)
    for half in range(ZH):
        out_ref[half * pairs : (half + 1) * pairs] = result
    rows.wait()


def order_kernel(data_ref, out_ref):
    rows = ZL * SLOTS // 2
    both = jnp.concatenate([data_ref[h * rows : (h + 1) * rows].reshape(2 * rows, LANES) for h in range(ZH)], axis=1)
    rows = jnp.dot(order_matrix(), both, preferred_element_type=jnp.float32).astype(jnp.bfloat16)
    for j in range(YC):
        for t in range(EXT_C // 2):
            for h in range(ZH):
                tile = rows[(2 * j + t) * TILE : (2 * j + t + 1) * TILE, h * LANES : (h + 1) * LANES]
                for x in range(XS):
                    out_ref[x * YC + j, (t * ZH + h) * TILE : (t * ZH + h + 1) * TILE, :] = tile


def image_kernel(data_ref, table_ref, out_ref):
    window = window_matrix()
    summed = []
    for x in range(XS):
        for h in range(ZH):
            slabs = []
            for t in range(EXT_C // 2):
                at = (t * ZH + h) * TILE
                slabs.append(jnp.concatenate([data_ref[x * YC + j, at : at + TILE, :] for j in range(YC)], axis=0))
            summed.append(jnp.dot(window, jnp.concatenate(slabs, axis=1), preferred_element_type=jnp.float32))
    first = lax.broadcasted_iota(jnp.int32, (SUBAP, LANES), 1) < HALF
    logs = []
    for c in range(EXT_C):
        at = (c // 2) * LANES
        lanes = []
        for st in range(0, STRIPS, 2):
            a = summed[st][:, at : at + LANES]
            b = summed[st + 1][:, at : at + LANES]
            if c % 2 == 0:
                both = jnp.where(first, a, pltpu.roll(b, HALF, 1))
            else:
                both = jnp.where(first, pltpu.roll(a, HALF, 1), b)
            lanes.append(both.astype(jnp.bfloat16))
        frames = lax.dot_general(
            table_ref[...],
            jnp.concatenate(lanes, axis=1),
            (((1,), (1,)), ((), ())),
            preferred_element_type=jnp.float32,
        )
        re, im = frames[:EXT_R], frames[EXT_R:]
        logs.append(jnp.log(1.0 + re * re + im * im))
    for c in range(OWN_C):
        column = logs[c] + logs[c + 1] + logs[c + 2]
        total = column[:OWN_R] + column[1 : OWN_R + 1] + column[2 : OWN_R + 2]
        filtered = total * (1.0 / 9.0)
        back = filtered
        for step in (1, 2, 4, 8):
            back = back + pltpu.roll(back, step, 1)
        out_ref[:, c, :] = filtered - back * (1.0 / BG)


def body(spectra, offsets):
    strip = (lax.axis_index("x") * ZH + lax.axis_index("zh")).reshape(1)
    vmem = pl.BlockSpec(memory_space=pltpu.VMEM)
    smem = pl.BlockSpec(memory_space=pltpu.SMEM)
    hbm = pl.BlockSpec(memory_space=pltpu.HBM)
    params = pltpu.CompilerParams(vmem_limit_bytes=VMEM_BYTES)
    columns = jnp.asarray(column_matrix())
    sent, rows = pl.pallas_call(
        columns_kernel,
        out_shape=[
            jax.ShapeDtypeStruct((ZH * ZL * SLOTS // 2, 2, LANES), jnp.bfloat16),
            jax.ShapeDtypeStruct((2 * EXT_R, 2 * KR), jnp.bfloat16),
        ],
        in_specs=[smem, hbm, hbm, hbm, hbm],
        out_specs=[vmem, vmem],
        scratch_shapes=[
            pltpu.SMEM(offsets.shape, jnp.int32),
            pltpu.VMEM(spectra.shape, jnp.bfloat16),
            pltpu.VMEM(columns.shape, jnp.bfloat16),
            pltpu.SemaphoreType.DMA((5,)),
        ],
        compiler_params=params,
    )(strip, *(pltpu.with_memory_space_constraint(a, pltpu.HBM) for a in (offsets, spectra, columns, jnp.asarray(row_matrices()))))
    got = lax.all_to_all(sent.reshape(ZH * ZL, SLOTS // 2, 2, LANES), ("zh", "zl"), 0, 0, tiled=True)
    sent = pl.pallas_call(
        order_kernel,
        out_shape=jax.ShapeDtypeStruct((XS * YC, EXT_C // 2 * ZH * TILE, LANES), jnp.bfloat16),
        in_specs=[vmem],
        out_specs=vmem,
        compiler_params=params,
    )(got.reshape(sent.shape))
    data = lax.all_to_all(sent, ("x", "y", "co"), 0, 0, tiled=True)
    return pl.pallas_call(
        image_kernel,
        out_shape=jax.ShapeDtypeStruct((OWN_R, OWN_C, SUBAP), jnp.float32),
        in_specs=[vmem, vmem],
        out_specs=vmem,
        compiler_params=params,
    )(data, rows)


def solution(mesh):
    grid = Mesh(mesh.devices.reshape(ZL, YC // 2, 2, XS, ZH), ("zl", "y", "co", "x", "zh"))
    in_specs = (P(("zl", "y", "co"), ("x", "zh"), None), P(("zl", "y", "co")))
    out_specs = P(("x", "zh"), ("zl", "y", "co"), None)
    return jax.shard_map(body, mesh=grid, in_specs=in_specs, out_specs=out_specs, check_vma=False)
```

```python
import math

import jax
import jax.numpy as jnp
import numpy as np
import ml_dtypes
from jax import lax
from jax.experimental import pallas as pl
from jax.experimental.pallas import tpu as pltpu
from jax.sharding import Mesh, PartitionSpec as P

KR = 256
KA = 1024
ROWS = 1024
COLS = 256
WIN = 8
BG = 16
SUBAP = 128
SUBS = 64
STRIPS = 8
OWN_S = SUBAP // SUBS
OWN_K = KR // STRIPS
OWN_C = COLS // SUBS
OWN_R = ROWS // STRIPS
EXT_C = OWN_C + 2
EXT_R = OWN_R + 8
VMEM_BYTES = 24 << 20
LANES = 128
HALF = 64
ZL, YC, XS, ZH = 8, 8, 4, 2
BLOCK = COLS // ZL
PAIRS = BLOCK // 2 + 1
SLOTS = BLOCK + 4
TILE = OWN_S * ZL


def column_matrix():
    n = np.arange(KA)[None, :]
    slot = np.arange(SLOTS)[None, :]
    col = (np.arange(ZL)[:, None] * BLOCK - 1 + slot).reshape(-1, 1)
    valid = np.broadcast_to(slot < BLOCK + 2, (ZL, SLOTS)).reshape(-1, 1) & (col >= 0) & (col < COLS)
    phase = ((n * col) % KA).astype(np.float64) * (2.0 * math.pi / KA)
    scale = valid / math.sqrt(KA)
    return np.stack([np.cos(phase) * scale, -np.sin(phase) * scale]).astype(ml_dtypes.bfloat16)


def row_matrices():
    scale = 1.0 / math.sqrt(KR)
    k = np.arange(KR)[None, :] - KR // 2
    out = np.zeros((STRIPS, 2, EXT_R, STRIPS, 2, OWN_K), np.float64)
    for strip in range(STRIPS):
        m = strip * OWN_R - 1 + np.arange(OWN_R + 2)
        valid = ((m >= 0) & (m < ROWS)).astype(np.float64)[:, None]
        phase = ((m[:, None] * k) % ROWS).astype(np.float64) * (2.0 * math.pi / ROWS)
        cosine = (np.cos(phase) * scale * valid).reshape(-1, STRIPS, OWN_K)
        sine = (np.sin(phase) * scale * valid).reshape(-1, STRIPS, OWN_K)
        n = OWN_R + 2
        out[strip, 0, :n, :, 0] = cosine
        out[strip, 0, :n, :, 1] = -sine
        out[strip, 1, :n, :, 0] = sine
        out[strip, 1, :n, :, 1] = cosine
    return out.reshape(STRIPS, 2 * EXT_R, 2 * KR).astype(ml_dtypes.bfloat16)


def window_matrix():
    frame = lax.broadcasted_iota(jnp.int32, (SUBAP, SUBAP), 0)
    lane = lax.broadcasted_iota(jnp.int32, (SUBAP, SUBAP), 1)
    sub = OWN_S * ((lane & (ZL - 1)) * YC + (lane >> 4)) + ((lane >> 3) & 1)
    return jnp.where(((sub - frame) & (SUBAP - 1)) < WIN, 1.0, 0.0).astype(jnp.bfloat16)


def order_matrix():
    row = lax.broadcasted_iota(jnp.int32, (PAIRS * TILE, ZL * SLOTS), 0)
    lane = lax.broadcasted_iota(jnp.int32, (PAIRS * TILE, ZL * SLOTS), 1)
    source = (row & (ZL - 1)) * SLOTS + (row >> 3)
    return jnp.where(source == lane, 1.0, 0.0).astype(jnp.bfloat16)


AXES = ("zl", "y", "co", "x", "zh")
FIRST_Z = 8
FIRST_X, FIRST_Y, FIRST_CO = 2, 2, 0


def place(x, y, co, z):
    zh, zl = z // ZL, z % ZL
    return (((zl * (YC // 2) + y) * 2 + co) * XS + x) * ZH + zh


def z_groups():
    zs = [(FIRST_Z + i) % (ZH * ZL) for i in range(ZH * ZL)]
    return [[place(x, y, co, z) for z in zs] for x in range(XS) for y in range(YC // 2) for co in range(2)]


def plane_order():
    return [
        ((FIRST_X + i) % XS, (FIRST_Y + j) % (YC // 2), (FIRST_CO + k) % 2)
        for i in range(XS)
        for j in range(YC // 2)
        for k in range(2)
    ]


def plane_groups():
    return [[place(*xyc, z) for xyc in plane_order()] for z in range(ZH * ZL)]


def columns_kernel(
    strip_ref, offsets_hbm, spectra_hbm, table_hbm, tables_hbm, out_ref, rows_ref, offsets_ref, spectra_ref, table_ref, arrived
):
    small = pltpu.make_async_copy(offsets_hbm, offsets_ref, arrived.at[0])
    whole = pltpu.make_async_copy(spectra_hbm, spectra_ref, arrived.at[1])
    rows = pltpu.make_async_copy(tables_hbm.at[strip_ref[0]], rows_ref, arrived.at[2])
    fetches = [pltpu.make_async_copy(table_hbm.at[i], table_ref.at[i], arrived.at[3 + i]) for i in range(2)]
    for fetch in [small, whole] + fetches + [rows]:
        fetch.start()
    small.wait()
    lane = lax.broadcasted_iota(jnp.int32, (8, LANES), 1)
    sample = (lane & (OWN_K - 1)) + strip_ref[0] * OWN_K - KR // 2
    offset = jnp.where(lane < HALF, offsets_ref[0], offsets_ref[1])
    angle = ((offset * sample) & (ROWS - 1)).astype(jnp.float32) * (2.0 * math.pi / ROWS)
    cosine = jnp.cos(angle)[:1]
    sine = jnp.sin(angle)
    sine = jnp.where((lane & OWN_K) == 0, -sine, sine)[:1]
    whole.wait()
    re = [spectra_ref[s, :, :KA] for s in range(OWN_S)]
    im = [spectra_ref[s, :, KA:] for s in range(OWN_S)]
    mixed = None
    for fetch, part in zip(fetches, (0, 1)):
        if part == 0:
            stack = jnp.concatenate([re[0], im[0], re[1], im[1]], axis=0)
        else:
            stack = jnp.concatenate([-im[0], re[0], -im[1], re[1]], axis=0)
        fetch.wait()
        product = lax.dot_general(table_ref[part], stack, (((1,), (1,)), ((), ())), preferred_element_type=jnp.float32)
        mixed = product if mixed is None else mixed + product
    lanes = lax.broadcasted_iota(jnp.int32, mixed.shape, 1)
    other = jnp.where((lanes & OWN_K) == 0, pltpu.roll(mixed, LANES - OWN_K, 1), pltpu.roll(mixed, OWN_K, 1))
    shifted = mixed * cosine + other * sine
    turned = pltpu.roll(shifted, HALF, 1)
    odd_row = lax.broadcasted_iota(jnp.int32, shifted.shape, 0) & 1
    partner = jnp.where(odd_row == 1, pltpu.roll(turned, 1, 0), pltpu.roll(turned, ZL * SLOTS - 1, 0))
    pairs = ZL * SLOTS // 2
    result = jnp.where(odd_row == lanes >> 6, shifted, partner).astype(jnp.bfloat16).reshape(pairs, 2, LANES)
    own = SLOTS // 2
    for g in range(ZH * ZL):
        z = (FIRST_Z + g) % ZL
        out_ref[g * own : (g + 1) * own] = result[z * own : (z + 1) * own]
    rows.wait()


def order_kernel(data_ref, out_ref):
    own = SLOTS // 2
    halves = []
    for h in range(ZH):
        at = [(h * ZL + z - FIRST_Z) % (ZH * ZL) * own for z in range(ZL)]
        halves.append(jnp.concatenate([data_ref[a : a + own] for a in at], axis=0).reshape(ZL * SLOTS, LANES))
    both = jnp.concatenate(halves, axis=1)
    rows = jnp.dot(order_matrix(), both, preferred_element_type=jnp.float32).astype(jnp.bfloat16)
    for to, (_, y, co) in enumerate(plane_order()):
        j = y * 2 + co
        for t in range(EXT_C // 2):
            for h in range(ZH):
                tile = rows[(2 * j + t) * TILE : (2 * j + t + 1) * TILE, h * LANES : (h + 1) * LANES]
                out_ref[to, (t * ZH + h) * TILE : (t * ZH + h + 1) * TILE, :] = tile


def image_kernel(data_ref, table_ref, out_ref):
    window = window_matrix()
    summed = []
    at_plane = {xyc: i for i, xyc in enumerate(plane_order())}
    for x in range(XS):
        for h in range(ZH):
            slabs = []
            for t in range(EXT_C // 2):
                at = (t * ZH + h) * TILE
                slabs.append(jnp.concatenate([data_ref[at_plane[x, j // 2, j % 2], at : at + TILE, :] for j in range(YC)], axis=0))
            summed.append(jnp.dot(window, jnp.concatenate(slabs, axis=1), preferred_element_type=jnp.float32))
    first = lax.broadcasted_iota(jnp.int32, (SUBAP, LANES), 1) < HALF
    logs = []
    for c in range(EXT_C):
        at = (c // 2) * LANES
        lanes = []
        for st in range(0, STRIPS, 2):
            a = summed[st][:, at : at + LANES]
            b = summed[st + 1][:, at : at + LANES]
            if c % 2 == 0:
                both = jnp.where(first, a, pltpu.roll(b, HALF, 1))
            else:
                both = jnp.where(first, pltpu.roll(a, HALF, 1), b)
            lanes.append(both.astype(jnp.bfloat16))
        frames = lax.dot_general(
            table_ref[...],
            jnp.concatenate(lanes, axis=1),
            (((1,), (1,)), ((), ())),
            preferred_element_type=jnp.float32,
        )
        re, im = frames[:EXT_R], frames[EXT_R:]
        logs.append(jnp.log(1.0 + re * re + im * im))
    for c in range(OWN_C):
        column = logs[c] + logs[c + 1] + logs[c + 2]
        total = column[:OWN_R] + column[1 : OWN_R + 1] + column[2 : OWN_R + 2]
        filtered = total * (1.0 / 9.0)
        back = filtered
        for step in (1, 2, 4, 8):
            back = back + pltpu.roll(back, step, 1)
        out_ref[:, c, :] = filtered - back * (1.0 / BG)


def body(spectra, offsets):
    strip = (lax.axis_index("x") * ZH + lax.axis_index("zh")).reshape(1)
    vmem = pl.BlockSpec(memory_space=pltpu.VMEM)
    smem = pl.BlockSpec(memory_space=pltpu.SMEM)
    hbm = pl.BlockSpec(memory_space=pltpu.HBM)
    params = pltpu.CompilerParams(vmem_limit_bytes=VMEM_BYTES)
    columns = jnp.asarray(column_matrix())
    sent, rows = pl.pallas_call(
        columns_kernel,
        out_shape=[
            jax.ShapeDtypeStruct((ZH * ZL * SLOTS // 2, 2, LANES), jnp.bfloat16),
            jax.ShapeDtypeStruct((2 * EXT_R, 2 * KR), jnp.bfloat16),
        ],
        in_specs=[smem, hbm, hbm, hbm, hbm],
        out_specs=[vmem, vmem],
        scratch_shapes=[
            pltpu.SMEM(offsets.shape, jnp.int32),
            pltpu.VMEM(spectra.shape, jnp.bfloat16),
            pltpu.VMEM(columns.shape, jnp.bfloat16),
            pltpu.SemaphoreType.DMA((5,)),
        ],
        compiler_params=params,
    )(strip, *(pltpu.with_memory_space_constraint(a, pltpu.HBM) for a in (offsets, spectra, columns, jnp.asarray(row_matrices()))))
    got = lax.all_to_all(sent.reshape(ZH * ZL, SLOTS // 2, 2, LANES), AXES, 0, 0, tiled=True, axis_index_groups=z_groups())
    sent = pl.pallas_call(
        order_kernel,
        out_shape=jax.ShapeDtypeStruct((XS * YC, EXT_C // 2 * ZH * TILE, LANES), jnp.bfloat16),
        in_specs=[vmem],
        out_specs=vmem,
        compiler_params=params,
    )(got.reshape(sent.shape))
    data = lax.all_to_all(sent, AXES, 0, 0, tiled=True, axis_index_groups=plane_groups())
    return pl.pallas_call(
        image_kernel,
        out_shape=jax.ShapeDtypeStruct((OWN_R, OWN_C, SUBAP), jnp.float32),
        in_specs=[vmem, vmem],
        out_specs=vmem,
        compiler_params=params,
    )(data, rows)


def solution(mesh):
    grid = Mesh(mesh.devices.reshape(ZL, YC // 2, 2, XS, ZH), ("zl", "y", "co", "x", "zh"))
    in_specs = (P(("zl", "y", "co"), ("x", "zh"), None), P(("zl", "y", "co")))
    out_specs = P(("x", "zh"), ("zl", "y", "co"), None)
    return jax.shard_map(body, mesh=grid, in_specs=in_specs, out_specs=out_specs, check_vma=False)
```

```python
import math

import jax
import jax.numpy as jnp
import numpy as np
import ml_dtypes
from jax import lax
from jax.experimental import pallas as pl
from jax.experimental.pallas import tpu as pltpu
from jax.sharding import Mesh, PartitionSpec as P

KR = 256
KA = 1024
ROWS = 1024
COLS = 256
WIN = 8
BG = 16
SUBAP = 128
SUBS = 64
STRIPS = 8
OWN_S = SUBAP // SUBS
OWN_K = KR // STRIPS
OWN_C = COLS // SUBS
OWN_R = ROWS // STRIPS
EXT_C = OWN_C + 2
EXT_R = OWN_R + 8
VMEM_BYTES = 24 << 20
LANES = 128
HALF = 64
ZL, YC, XS, ZH = 8, 8, 4, 2
BLOCK = COLS // ZL
PAIRS = BLOCK // 2 + 1
SLOTS = BLOCK + 4
TILE = OWN_S * ZL


def column_matrix():
    n = np.arange(KA // 2)[None, :]
    slot = np.arange(SLOTS)[None, :]
    col = (np.arange(ZL)[:, None] * BLOCK - 1 + slot).reshape(-1, 1)
    valid = np.broadcast_to(slot < BLOCK + 2, (ZL, SLOTS)).reshape(-1, 1) & (col >= 0) & (col < COLS)
    phase = ((n * col) % KA).astype(np.float64) * (2.0 * math.pi / KA)
    scale = valid / math.sqrt(KA)
    return np.stack([np.cos(phase) * scale, -np.sin(phase) * scale]).astype(ml_dtypes.bfloat16)


def row_matrices():
    scale = 1.0 / math.sqrt(KR)
    k = np.arange(KR)[None, :] - KR // 2
    out = np.zeros((STRIPS, 2, EXT_R, STRIPS, 2, OWN_K), np.float64)
    for strip in range(STRIPS):
        m = strip * OWN_R - 1 + np.arange(OWN_R + 2)
        valid = ((m >= 0) & (m < ROWS)).astype(np.float64)[:, None]
        phase = ((m[:, None] * k) % ROWS).astype(np.float64) * (2.0 * math.pi / ROWS)
        cosine = (np.cos(phase) * scale * valid).reshape(-1, STRIPS, OWN_K)
        sine = (np.sin(phase) * scale * valid).reshape(-1, STRIPS, OWN_K)
        n = OWN_R + 2
        out[strip, 0, :n, :, 0] = cosine
        out[strip, 0, :n, :, 1] = -sine
        out[strip, 1, :n, :, 0] = sine
        out[strip, 1, :n, :, 1] = cosine
    return out.reshape(STRIPS, 2 * EXT_R, 2 * KR).astype(ml_dtypes.bfloat16)


def window_matrix():
    frame = lax.broadcasted_iota(jnp.int32, (SUBAP, SUBAP), 0)
    lane = lax.broadcasted_iota(jnp.int32, (SUBAP, SUBAP), 1)
    sub = OWN_S * ((lane & (ZL - 1)) * YC + (lane >> 4)) + ((lane >> 3) & 1)
    return jnp.where(((sub - frame) & (SUBAP - 1)) < WIN, 1.0, 0.0).astype(jnp.bfloat16)


def order_matrix():
    row = lax.broadcasted_iota(jnp.int32, (PAIRS * TILE, ZL * SLOTS), 0)
    lane = lax.broadcasted_iota(jnp.int32, (PAIRS * TILE, ZL * SLOTS), 1)
    source = (row & (ZL - 1)) * SLOTS + (row >> 3)
    return jnp.where(source == lane, 1.0, 0.0).astype(jnp.bfloat16)


AXES = ("zl", "y", "co", "x", "zh")
Z_ORDER = (11, 12, 13, 14, 15, 0, 1, 2, 3, 4, 5, 6, 7, 8, 9, 10)
PLANE_ORDER = ((2, 2, 1), (2, 2, 0), (2, 3, 0), (2, 1, 0), (3, 2, 0), (1, 2, 0), (2, 0, 0), (3, 3, 0), (3, 1, 0), (0, 2, 0), (1, 3, 0), (1, 1, 0), (3, 0, 0), (0, 3, 0), (0, 1, 0), (1, 0, 0), (0, 0, 0), (2, 3, 1), (2, 1, 1), (3, 2, 1), (1, 2, 1), (2, 0, 1), (3, 3, 1), (3, 1, 1), (0, 2, 1), (1, 3, 1), (1, 1, 1), (3, 0, 1), (0, 3, 1), (0, 1, 1), (1, 0, 1), (0, 0, 1))


def place(x, y, co, z):
    zh, zl = z // ZL, z % ZL
    return (((zl * (YC // 2) + y) * 2 + co) * XS + x) * ZH + zh


def z_groups():
    return [[place(x, y, co, z) for z in Z_ORDER] for x in range(XS) for y in range(YC // 2) for co in range(2)]


def plane_order():
    return PLANE_ORDER


def plane_groups():
    return [[place(*xyc, z) for xyc in PLANE_ORDER] for z in range(ZH * ZL)]


def columns_kernel(
    strip_ref, offsets_hbm, spectra_hbm, table_hbm, tables_hbm, out_ref, rows_ref, offsets_ref, spectra_ref, table_ref, arrived
):
    small = pltpu.make_async_copy(offsets_hbm, offsets_ref, arrived.at[0])
    whole = pltpu.make_async_copy(spectra_hbm, spectra_ref, arrived.at[1])
    rows = pltpu.make_async_copy(tables_hbm.at[strip_ref[0]], rows_ref, arrived.at[2])
    fetches = [pltpu.make_async_copy(table_hbm.at[i], table_ref.at[i], arrived.at[3 + i]) for i in range(2)]
    for fetch in [small, whole] + fetches + [rows]:
        fetch.start()
    small.wait()
    lane = lax.broadcasted_iota(jnp.int32, (8, LANES), 1)
    sample = (lane & (OWN_K - 1)) + strip_ref[0] * OWN_K - KR // 2
    offset = jnp.where(lane < HALF, offsets_ref[0], offsets_ref[1])
    angle = ((offset * sample) & (ROWS - 1)).astype(jnp.float32) * (2.0 * math.pi / ROWS)
    cosine = jnp.cos(angle)[:1]
    sine = jnp.sin(angle)
    sine = jnp.where((lane & OWN_K) == 0, -sine, sine)[:1]
    whole.wait()
    re = [spectra_ref[s, :, :KA] for s in range(OWN_S)]
    im = [spectra_ref[s, :, KA:] for s in range(OWN_S)]
    mixed = None
    for fetch, part in zip(fetches, (0, 1)):
        sides = (re[0], im[0], re[1], im[1]) if part == 0 else (-im[0], re[0], -im[1], re[1])
        stack = jnp.concatenate([a[:, : KA // 2] for a in sides] + [a[:, KA // 2 :] for a in sides], axis=0)
        fetch.wait()
        product = lax.dot_general(table_ref[part], stack, (((1,), (1,)), ((), ())), preferred_element_type=jnp.float32)
        mixed = product if mixed is None else mixed + product
    odd_row = lax.broadcasted_iota(jnp.int32, (ZL * SLOTS, LANES), 0) & 1
    mixed = mixed[:, :LANES] + jnp.where(odd_row == 1, mixed[:, LANES:], -mixed[:, LANES:])
    lanes = lax.broadcasted_iota(jnp.int32, mixed.shape, 1)
    other = jnp.where((lanes & OWN_K) == 0, pltpu.roll(mixed, LANES - OWN_K, 1), pltpu.roll(mixed, OWN_K, 1))
    shifted = mixed * cosine + other * sine
    turned = pltpu.roll(shifted, HALF, 1)
    partner = jnp.where(odd_row == 1, pltpu.roll(turned, 1, 0), pltpu.roll(turned, ZL * SLOTS - 1, 0))
    pairs = ZL * SLOTS // 2
    result = jnp.where(odd_row == lanes >> 6, shifted, partner).astype(jnp.bfloat16).reshape(pairs, 2, LANES)
    own = SLOTS // 2
    for g in range(ZH * ZL):
        z = Z_ORDER[g] % ZL
        out_ref[g * own : (g + 1) * own] = result[z * own : (z + 1) * own]
    rows.wait()


def order_kernel(data_ref, out_ref):
    own = SLOTS // 2
    halves = []
    for h in range(ZH):
        at = [Z_ORDER.index(h * ZL + z) * own for z in range(ZL)]
        halves.append(jnp.concatenate([data_ref[a : a + own] for a in at], axis=0).reshape(ZL * SLOTS, LANES))
    both = jnp.concatenate(halves, axis=1)
    rows = jnp.dot(order_matrix(), both, preferred_element_type=jnp.float32).astype(jnp.bfloat16)
    for to, (_, y, co) in enumerate(plane_order()):
        j = y * 2 + co
        for t in range(EXT_C // 2):
            for h in range(ZH):
                tile = rows[(2 * j + t) * TILE : (2 * j + t + 1) * TILE, h * LANES : (h + 1) * LANES]
                out_ref[to, (t * ZH + h) * TILE : (t * ZH + h + 1) * TILE, :] = tile


def image_kernel(data_ref, table_ref, out_ref):
    window = window_matrix()
    summed = []
    at_plane = {xyc: i for i, xyc in enumerate(plane_order())}
    for x in range(XS):
        for h in range(ZH):
            slabs = []
            for t in range(EXT_C // 2):
                at = (t * ZH + h) * TILE
                slabs.append(jnp.concatenate([data_ref[at_plane[x, j // 2, j % 2], at : at + TILE, :] for j in range(YC)], axis=0))
            summed.append(jnp.dot(window, jnp.concatenate(slabs, axis=1), preferred_element_type=jnp.float32))
    first = lax.broadcasted_iota(jnp.int32, (SUBAP, LANES), 1) < HALF
    logs = []
    for t in range(EXT_C // 2):
        at = t * LANES
        columns = ([], [])
        for st in range(0, STRIPS, 2):
            a = summed[st][:, at : at + LANES]
            b = summed[st + 1][:, at : at + LANES]
            columns[0].append(jnp.where(first, a, pltpu.roll(b, HALF, 1)).astype(jnp.bfloat16))
            columns[1].append(jnp.where(first, pltpu.roll(a, HALF, 1), b).astype(jnp.bfloat16))
        both = jnp.concatenate([jnp.concatenate(column, axis=1) for column in columns], axis=0)
        frames = lax.dot_general(table_ref[...], both, (((1,), (1,)), ((), ())), preferred_element_type=jnp.float32)
        power = frames[:EXT_R] * frames[:EXT_R] + frames[EXT_R:] * frames[EXT_R:]
        power = jnp.log(1.0 + power)
        logs += [power[:, :SUBAP], power[:, SUBAP:]]
    for c in range(OWN_C):
        column = logs[c] + logs[c + 1] + logs[c + 2]
        total = column[:OWN_R] + column[1 : OWN_R + 1] + column[2 : OWN_R + 2]
        filtered = total * (1.0 / 9.0)
        back = filtered
        for step in (1, 2, 4, 8):
            back = back + pltpu.roll(back, step, 1)
        out_ref[:, c, :] = filtered - back * (1.0 / BG)


def body(spectra, offsets):
    strip = (lax.axis_index("x") * ZH + lax.axis_index("zh")).reshape(1)
    vmem = pl.BlockSpec(memory_space=pltpu.VMEM)
    smem = pl.BlockSpec(memory_space=pltpu.SMEM)
    hbm = pl.BlockSpec(memory_space=pltpu.HBM)
    params = pltpu.CompilerParams(vmem_limit_bytes=VMEM_BYTES)
    columns = jnp.asarray(column_matrix())
    sent, rows = pl.pallas_call(
        columns_kernel,
        out_shape=[
            jax.ShapeDtypeStruct((ZH * ZL * SLOTS // 2, 2, LANES), jnp.bfloat16),
            jax.ShapeDtypeStruct((2 * EXT_R, 2 * KR), jnp.bfloat16),
        ],
        in_specs=[smem, hbm, hbm, hbm, hbm],
        out_specs=[vmem, vmem],
        scratch_shapes=[
            pltpu.SMEM(offsets.shape, jnp.int32),
            pltpu.VMEM(spectra.shape, jnp.bfloat16),
            pltpu.VMEM(columns.shape, jnp.bfloat16),
            pltpu.SemaphoreType.DMA((5,)),
        ],
        compiler_params=params,
    )(strip, *(pltpu.with_memory_space_constraint(a, pltpu.HBM) for a in (offsets, spectra, columns, jnp.asarray(row_matrices()))))
    got = lax.all_to_all(sent.reshape(ZH * ZL, SLOTS // 2, 2, LANES), AXES, 0, 0, tiled=True, axis_index_groups=z_groups())
    sent = pl.pallas_call(
        order_kernel,
        out_shape=jax.ShapeDtypeStruct((XS * YC, EXT_C // 2 * ZH * TILE, LANES), jnp.bfloat16),
        in_specs=[vmem],
        out_specs=vmem,
        compiler_params=params,
    )(got.reshape(sent.shape))
    data = lax.all_to_all(sent, AXES, 0, 0, tiled=True, axis_index_groups=plane_groups())
    return pl.pallas_call(
        image_kernel,
        out_shape=jax.ShapeDtypeStruct((OWN_R, OWN_C, SUBAP), jnp.float32),
        in_specs=[vmem, vmem],
        out_specs=vmem,
        compiler_params=params,
    )(data, rows)


def solution(mesh):
    grid = Mesh(mesh.devices.reshape(ZL, YC // 2, 2, XS, ZH), ("zl", "y", "co", "x", "zh"))
    in_specs = (P(("zl", "y", "co"), ("x", "zh"), None), P(("zl", "y", "co")))
    out_specs = P(("x", "zh"), ("zl", "y", "co"), None)
    return jax.shard_map(body, mesh=grid, in_specs=in_specs, out_specs=out_specs, check_vma=False)
```

```python
import math

import jax
import jax.numpy as jnp
import numpy as np
import ml_dtypes
from jax import lax
from jax.experimental import pallas as pl
from jax.experimental.pallas import tpu as pltpu
from jax.sharding import Mesh, PartitionSpec as P

KR = 256
KA = 1024
ROWS = 1024
COLS = 256
WIN = 8
BG = 16
SUBAP = 128
SUBS = 64
STRIPS = 8
OWN_S = SUBAP // SUBS
OWN_K = KR // STRIPS
OWN_C = COLS // SUBS
OWN_R = ROWS // STRIPS
EXT_C = OWN_C + 2
EXT_R = OWN_R + 8
VMEM_BYTES = 24 << 20
LANES = 128
HALF = 64
ZL, YC, XS, ZH = 8, 8, 4, 2
BLOCK = COLS // ZL
PAIRS = BLOCK // 2 + 1
SLOTS = BLOCK + 2
TILE = OWN_S * ZL


def column_matrix():
    n = np.arange(KA // 2)[None, :]
    slot = np.arange(SLOTS)[None, :]
    col = (np.arange(ZL)[:, None] * BLOCK - 1 + slot).reshape(-1, 1)
    valid = np.broadcast_to(slot < BLOCK + 2, (ZL, SLOTS)).reshape(-1, 1) & (col >= 0) & (col < COLS)
    phase = ((n * col) % KA).astype(np.float64) * (2.0 * math.pi / KA)
    scale = valid / math.sqrt(KA)
    return np.stack([np.cos(phase) * scale, -np.sin(phase) * scale]).astype(ml_dtypes.bfloat16)


def row_matrices():
    scale = 1.0 / math.sqrt(KR)
    k = np.arange(KR)[None, :] - KR // 2
    out = np.zeros((STRIPS, 2, EXT_R, STRIPS, 2, OWN_K), np.float64)
    for strip in range(STRIPS):
        m = strip * OWN_R - 1 + np.arange(OWN_R + 2)
        valid = ((m >= 0) & (m < ROWS)).astype(np.float64)[:, None]
        phase = ((m[:, None] * k) % ROWS).astype(np.float64) * (2.0 * math.pi / ROWS)
        cosine = (np.cos(phase) * scale * valid).reshape(-1, STRIPS, OWN_K)
        sine = (np.sin(phase) * scale * valid).reshape(-1, STRIPS, OWN_K)
        n = OWN_R + 2
        out[strip, 0, :n, :, 0] = cosine
        out[strip, 0, :n, :, 1] = -sine
        out[strip, 1, :n, :, 0] = sine
        out[strip, 1, :n, :, 1] = cosine
    return out.reshape(STRIPS, 2 * EXT_R, 2 * KR).astype(ml_dtypes.bfloat16)


def window_matrix():
    frame = lax.broadcasted_iota(jnp.int32, (SUBAP, SUBAP), 0)
    lane = lax.broadcasted_iota(jnp.int32, (SUBAP, SUBAP), 1)
    sub = OWN_S * ((lane & (ZL - 1)) * YC + (lane >> 4)) + ((lane >> 3) & 1)
    return jnp.where(((sub - frame) & (SUBAP - 1)) < WIN, 1.0, 0.0).astype(jnp.bfloat16)


def order_matrix():
    row = lax.broadcasted_iota(jnp.int32, (PAIRS * TILE, ZL * SLOTS), 0)
    lane = lax.broadcasted_iota(jnp.int32, (PAIRS * TILE, ZL * SLOTS), 1)
    source = (row & (ZL - 1)) * SLOTS + (row >> 3)
    return jnp.where(source == lane, 1.0, 0.0).astype(jnp.bfloat16)


AXES = ("zl", "y", "co", "x", "zh")
Z_ORDER = (11, 12, 13, 14, 15, 0, 1, 2, 3, 4, 5, 6, 7, 8, 9, 10)
PLANE_ORDER = ((2, 2, 1), (2, 2, 0), (2, 3, 0), (2, 1, 0), (3, 2, 0), (1, 2, 0), (2, 0, 0), (3, 3, 0), (3, 1, 0), (0, 2, 0), (1, 3, 0), (1, 1, 0), (3, 0, 0), (0, 3, 0), (0, 1, 0), (1, 0, 0), (0, 0, 0), (2, 3, 1), (2, 1, 1), (3, 2, 1), (1, 2, 1), (2, 0, 1), (3, 3, 1), (3, 1, 1), (0, 2, 1), (1, 3, 1), (1, 1, 1), (3, 0, 1), (0, 3, 1), (0, 1, 1), (1, 0, 1), (0, 0, 1))


def place(x, y, co, z):
    zh, zl = z // ZL, z % ZL
    return (((zl * (YC // 2) + y) * 2 + co) * XS + x) * ZH + zh


def z_groups():
    return [[place(x, y, co, z) for z in Z_ORDER] for x in range(XS) for y in range(YC // 2) for co in range(2)]


def plane_order():
    return PLANE_ORDER


def plane_groups():
    return [[place(*xyc, z) for xyc in PLANE_ORDER] for z in range(ZH * ZL)]


def columns_kernel(
    strip_ref, offsets_hbm, spectra_hbm, table_hbm, tables_hbm, out_ref, rows_ref, offsets_ref, spectra_ref, table_ref, arrived
):
    small = pltpu.make_async_copy(offsets_hbm, offsets_ref, arrived.at[0])
    whole = pltpu.make_async_copy(spectra_hbm, spectra_ref, arrived.at[1])
    rows = pltpu.make_async_copy(tables_hbm.at[strip_ref[0]], rows_ref, arrived.at[2])
    fetches = [pltpu.make_async_copy(table_hbm.at[i], table_ref.at[i], arrived.at[3 + i]) for i in range(2)]
    for fetch in [small, whole] + fetches + [rows]:
        fetch.start()
    small.wait()
    lane = lax.broadcasted_iota(jnp.int32, (8, LANES), 1)
    sample = (lane & (OWN_K - 1)) + strip_ref[0] * OWN_K - KR // 2
    offset = jnp.where(lane < HALF, offsets_ref[0], offsets_ref[1])
    angle = ((offset * sample) & (ROWS - 1)).astype(jnp.float32) * (2.0 * math.pi / ROWS)
    cosine = jnp.cos(angle)[:1]
    sine = jnp.sin(angle)
    sine = jnp.where((lane & OWN_K) == 0, -sine, sine)[:1]
    whole.wait()
    re = [spectra_ref[s, :, :KA] for s in range(OWN_S)]
    im = [spectra_ref[s, :, KA:] for s in range(OWN_S)]
    mixed = None
    for fetch, part in zip(fetches, (0, 1)):
        sides = (re[0], im[0], re[1], im[1]) if part == 0 else (-im[0], re[0], -im[1], re[1])
        stack = jnp.concatenate([a[:, : KA // 2] for a in sides] + [a[:, KA // 2 :] for a in sides], axis=0)
        fetch.wait()
        product = lax.dot_general(table_ref[part], stack, (((1,), (1,)), ((), ())), preferred_element_type=jnp.float32)
        mixed = product if mixed is None else mixed + product
    odd_row = lax.broadcasted_iota(jnp.int32, (ZL * SLOTS, LANES), 0) & 1
    mixed = mixed[:, :LANES] + jnp.where(odd_row == 1, mixed[:, LANES:], -mixed[:, LANES:])
    lanes = lax.broadcasted_iota(jnp.int32, mixed.shape, 1)
    other = jnp.where((lanes & OWN_K) == 0, pltpu.roll(mixed, LANES - OWN_K, 1), pltpu.roll(mixed, OWN_K, 1))
    shifted = mixed * cosine + other * sine
    turned = pltpu.roll(shifted, HALF, 1)
    partner = jnp.where(odd_row == 1, pltpu.roll(turned, 1, 0), pltpu.roll(turned, ZL * SLOTS - 1, 0))
    pairs = ZL * SLOTS // 2
    result = jnp.where(odd_row == lanes >> 6, shifted, partner).astype(jnp.bfloat16).reshape(pairs, 2, LANES)
    own = SLOTS // 2
    for g in range(ZH * ZL):
        z = Z_ORDER[g] % ZL
        out_ref[g * own : (g + 1) * own] = result[z * own : (z + 1) * own]
    rows.wait()


def order_kernel(data_ref, out_ref):
    own = SLOTS // 2
    halves = []
    for h in range(ZH):
        at = [Z_ORDER.index(h * ZL + z) * own for z in range(ZL)]
        halves.append(jnp.concatenate([data_ref[a : a + own] for a in at], axis=0).reshape(ZL * SLOTS, LANES))
    both = jnp.concatenate(halves, axis=1)
    rows = jnp.dot(order_matrix(), both, preferred_element_type=jnp.float32).astype(jnp.bfloat16)
    for to, (_, y, co) in enumerate(plane_order()):
        j = y * 2 + co
        for t in range(EXT_C // 2):
            for h in range(ZH):
                tile = rows[(2 * j + t) * TILE : (2 * j + t + 1) * TILE, h * LANES : (h + 1) * LANES]
                out_ref[to, (t * ZH + h) * TILE : (t * ZH + h + 1) * TILE, :] = tile


def image_kernel(data_ref, table_ref, out_ref):
    window = window_matrix()
    summed = []
    at_plane = {xyc: i for i, xyc in enumerate(plane_order())}
    for x in range(XS):
        for h in range(ZH):
            slabs = []
            for t in range(EXT_C // 2):
                at = (t * ZH + h) * TILE
                slabs.append(jnp.concatenate([data_ref[at_plane[x, j // 2, j % 2], at : at + TILE, :] for j in range(YC)], axis=0))
            summed.append(jnp.dot(window, jnp.concatenate(slabs, axis=1), preferred_element_type=jnp.float32))
    logs = []
    for t in range(EXT_C // 2):
        at = t * LANES
        columns = ([], [])
        for st in range(0, STRIPS, 2):
            a = summed[st][:, at : at + LANES]
            b = summed[st + 1][:, at : at + LANES]
            a, b = a.astype(jnp.bfloat16), b.astype(jnp.bfloat16)
            columns[0].append(jnp.concatenate([a[:, :HALF], b[:, :HALF]], axis=1))
            columns[1].append(jnp.concatenate([a[:, HALF:], b[:, HALF:]], axis=1))
        both = jnp.concatenate([jnp.concatenate(column, axis=1) for column in columns], axis=0)
        frames = lax.dot_general(table_ref[...], both, (((1,), (1,)), ((), ())), preferred_element_type=jnp.float32)
        power = frames[:EXT_R] * frames[:EXT_R] + frames[EXT_R:] * frames[EXT_R:]
        power = jnp.log(1.0 + power)
        logs += [power[:, :SUBAP], power[:, SUBAP:]]
    for c in range(OWN_C):
        column = logs[c] + logs[c + 1] + logs[c + 2]
        total = column[:OWN_R] + column[1 : OWN_R + 1] + column[2 : OWN_R + 2]
        filtered = total * (1.0 / 9.0)
        back = filtered
        for step in (1, 2, 4, 8):
            back = back + pltpu.roll(back, step, 1)
        out_ref[:, c, :] = filtered - back * (1.0 / BG)


def body(spectra, offsets):
    strip = (lax.axis_index("x") * ZH + lax.axis_index("zh")).reshape(1)
    vmem = pl.BlockSpec(memory_space=pltpu.VMEM)
    smem = pl.BlockSpec(memory_space=pltpu.SMEM)
    hbm = pl.BlockSpec(memory_space=pltpu.HBM)
    params = pltpu.CompilerParams(vmem_limit_bytes=VMEM_BYTES)
    columns = jnp.asarray(column_matrix())
    sent, rows = pl.pallas_call(
        columns_kernel,
        out_shape=[
            jax.ShapeDtypeStruct((ZH * ZL * SLOTS // 2, 2, LANES), jnp.bfloat16),
            jax.ShapeDtypeStruct((2 * EXT_R, 2 * KR), jnp.bfloat16),
        ],
        in_specs=[smem, hbm, hbm, hbm, hbm],
        out_specs=[vmem, vmem],
        scratch_shapes=[
            pltpu.SMEM(offsets.shape, jnp.int32),
            pltpu.VMEM(spectra.shape, jnp.bfloat16),
            pltpu.VMEM(columns.shape, jnp.bfloat16),
            pltpu.SemaphoreType.DMA((5,)),
        ],
        compiler_params=params,
    )(strip, *(pltpu.with_memory_space_constraint(a, pltpu.HBM) for a in (offsets, spectra, columns, jnp.asarray(row_matrices()))))
    got = lax.all_to_all(sent.reshape(ZH * ZL, SLOTS // 2, 2, LANES), AXES, 0, 0, tiled=True, axis_index_groups=z_groups())
    sent = pl.pallas_call(
        order_kernel,
        out_shape=jax.ShapeDtypeStruct((XS * YC, EXT_C // 2 * ZH * TILE, LANES), jnp.bfloat16),
        in_specs=[vmem],
        out_specs=vmem,
        compiler_params=params,
    )(got.reshape(sent.shape))
    data = lax.all_to_all(sent, AXES, 0, 0, tiled=True, axis_index_groups=plane_groups())
    return pl.pallas_call(
        image_kernel,
        out_shape=jax.ShapeDtypeStruct((OWN_R, OWN_C, SUBAP), jnp.float32),
        in_specs=[vmem, vmem],
        out_specs=vmem,
        compiler_params=params,
    )(data, rows)


def solution(mesh):
    grid = Mesh(mesh.devices.reshape(ZL, YC // 2, 2, XS, ZH), ("zl", "y", "co", "x", "zh"))
    in_specs = (P(("zl", "y", "co"), ("x", "zh"), None), P(("zl", "y", "co")))
    out_specs = P(("x", "zh"), ("zl", "y", "co"), None)
    return jax.shard_map(body, mesh=grid, in_specs=in_specs, out_specs=out_specs, check_vma=False)
```

```python
import math

import jax
import jax.numpy as jnp
import numpy as np
import ml_dtypes
from jax import lax
from jax.experimental import pallas as pl
from jax.experimental.pallas import tpu as pltpu
from jax.sharding import Mesh, PartitionSpec as P

KR = 256
KA = 1024
ROWS = 1024
COLS = 256
WIN = 8
BG = 16
SUBAP = 128
SUBS = 64
STRIPS = 8
OWN_S = SUBAP // SUBS
OWN_K = KR // STRIPS
OWN_C = COLS // SUBS
OWN_R = ROWS // STRIPS
EXT_C = OWN_C + 2
EXT_R = OWN_R + 8
VMEM_BYTES = 24 << 20
LANES = 128
HALF = 64
ZL, YC, XS, ZH = 8, 8, 4, 2
BLOCK = COLS // ZL
PAIRS = BLOCK // 2 + 1
SLOTS = BLOCK + 2
TILE = OWN_S * ZL


def column_matrix():
    n = np.arange(KA // 2)[None, :]
    slot = np.arange(SLOTS)[None, :]
    col = (np.arange(ZL)[:, None] * BLOCK - 1 + slot).reshape(-1, 1)
    valid = np.broadcast_to(slot < BLOCK + 2, (ZL, SLOTS)).reshape(-1, 1) & (col >= 0) & (col < COLS)
    phase = ((n * col) % KA).astype(np.float64) * (2.0 * math.pi / KA)
    scale = valid / math.sqrt(KA)
    return np.stack([np.cos(phase) * scale, -np.sin(phase) * scale]).astype(ml_dtypes.bfloat16)


def row_matrices():
    scale = 1.0 / math.sqrt(KR)
    k = np.arange(KR)[None, :] - KR // 2
    out = np.zeros((STRIPS, 2, EXT_R, STRIPS, 2, OWN_K), np.float64)
    for strip in range(STRIPS):
        m = strip * OWN_R - 1 + np.arange(OWN_R + 2)
        valid = ((m >= 0) & (m < ROWS)).astype(np.float64)[:, None]
        phase = ((m[:, None] * k) % ROWS).astype(np.float64) * (2.0 * math.pi / ROWS)
        cosine = (np.cos(phase) * scale * valid).reshape(-1, STRIPS, OWN_K)
        sine = (np.sin(phase) * scale * valid).reshape(-1, STRIPS, OWN_K)
        n = OWN_R + 2
        out[strip, 0, :n, :, 0] = cosine
        out[strip, 0, :n, :, 1] = -sine
        out[strip, 1, :n, :, 0] = sine
        out[strip, 1, :n, :, 1] = cosine
    return out.reshape(STRIPS, 2 * EXT_R, 2 * KR).astype(ml_dtypes.bfloat16)


def window_matrix():
    frame = lax.broadcasted_iota(jnp.int32, (SUBAP, SUBAP), 0)
    lane = lax.broadcasted_iota(jnp.int32, (SUBAP, SUBAP), 1)
    sub = OWN_S * ((lane & (ZL - 1)) * YC + (lane >> 4)) + ((lane >> 3) & 1)
    return jnp.where(((sub - frame) & (SUBAP - 1)) < WIN, 1.0, 0.0).astype(jnp.bfloat16)


def background_matrix():
    source = lax.broadcasted_iota(jnp.int32, (SUBAP, SUBAP), 0)
    frame = lax.broadcasted_iota(jnp.int32, (SUBAP, SUBAP), 1)
    mean = jnp.where(((frame - source) & (SUBAP - 1)) < BG, 1.0 / BG, 0.0)
    return (jnp.where(source == frame, 1.0, 0.0) - mean).astype(jnp.bfloat16)


def order_matrix():
    row = lax.broadcasted_iota(jnp.int32, (PAIRS * TILE, ZL * SLOTS), 0)
    lane = lax.broadcasted_iota(jnp.int32, (PAIRS * TILE, ZL * SLOTS), 1)
    source = (row & (ZL - 1)) * SLOTS + (row >> 3)
    return jnp.where(source == lane, 1.0, 0.0).astype(jnp.bfloat16)


AXES = ("zl", "y", "co", "x", "zh")
Z_ORDER = (11, 12, 13, 14, 15, 0, 1, 2, 3, 4, 5, 6, 7, 8, 9, 10)
PLANE_ORDER = ((2, 2, 1), (2, 2, 0), (2, 3, 0), (2, 1, 0), (3, 2, 0), (1, 2, 0), (2, 0, 0), (3, 3, 0), (3, 1, 0), (0, 2, 0), (1, 3, 0), (1, 1, 0), (3, 0, 0), (0, 3, 0), (0, 1, 0), (1, 0, 0), (0, 0, 0), (2, 3, 1), (2, 1, 1), (3, 2, 1), (1, 2, 1), (2, 0, 1), (3, 3, 1), (3, 1, 1), (0, 2, 1), (1, 3, 1), (1, 1, 1), (3, 0, 1), (0, 3, 1), (0, 1, 1), (1, 0, 1), (0, 0, 1))


def place(x, y, co, z):
    zh, zl = z // ZL, z % ZL
    return (((zl * (YC // 2) + y) * 2 + co) * XS + x) * ZH + zh


def z_groups():
    return [[place(x, y, co, z) for z in Z_ORDER] for x in range(XS) for y in range(YC // 2) for co in range(2)]


def plane_order():
    return PLANE_ORDER


def plane_groups():
    return [[place(*xyc, z) for xyc in PLANE_ORDER] for z in range(ZH * ZL)]


def columns_kernel(
    strip_ref, offsets_hbm, spectra_hbm, table_hbm, tables_hbm, out_ref, rows_ref, offsets_ref, spectra_ref, table_ref, arrived
):
    small = pltpu.make_async_copy(offsets_hbm, offsets_ref, arrived.at[0])
    whole = pltpu.make_async_copy(spectra_hbm, spectra_ref, arrived.at[1])
    rows = pltpu.make_async_copy(tables_hbm.at[strip_ref[0]], rows_ref, arrived.at[2])
    fetches = [pltpu.make_async_copy(table_hbm.at[i], table_ref.at[i], arrived.at[3 + i]) for i in range(2)]
    for fetch in [small, whole] + fetches + [rows]:
        fetch.start()
    small.wait()
    lane = lax.broadcasted_iota(jnp.int32, (8, LANES), 1)
    sample = (lane & (OWN_K - 1)) + strip_ref[0] * OWN_K - KR // 2
    offset = jnp.where(lane < HALF, offsets_ref[0], offsets_ref[1])
    angle = ((offset * sample) & (ROWS - 1)).astype(jnp.float32) * (2.0 * math.pi / ROWS)
    cosine = jnp.cos(angle)[:1]
    sine = jnp.sin(angle)
    sine = jnp.where((lane & OWN_K) == 0, -sine, sine)[:1]
    whole.wait()
    re = [spectra_ref[s, :, :KA] for s in range(OWN_S)]
    im = [spectra_ref[s, :, KA:] for s in range(OWN_S)]
    mixed = None
    for fetch, part in zip(fetches, (0, 1)):
        sides = (re[0], im[0], re[1], im[1]) if part == 0 else (-im[0], re[0], -im[1], re[1])
        stack = jnp.concatenate([a[:, : KA // 2] for a in sides] + [a[:, KA // 2 :] for a in sides], axis=0)
        fetch.wait()
        product = lax.dot_general(table_ref[part], stack, (((1,), (1,)), ((), ())), preferred_element_type=jnp.float32)
        mixed = product if mixed is None else mixed + product
    odd_row = lax.broadcasted_iota(jnp.int32, (ZL * SLOTS, LANES), 0) & 1
    mixed = mixed[:, :LANES] + jnp.where(odd_row == 1, mixed[:, LANES:], -mixed[:, LANES:])
    lanes = lax.broadcasted_iota(jnp.int32, mixed.shape, 1)
    other = jnp.where((lanes & OWN_K) == 0, pltpu.roll(mixed, LANES - OWN_K, 1), pltpu.roll(mixed, OWN_K, 1))
    shifted = mixed * cosine + other * sine
    turned = pltpu.roll(shifted, HALF, 1)
    partner = jnp.where(odd_row == 1, pltpu.roll(turned, 1, 0), pltpu.roll(turned, ZL * SLOTS - 1, 0))
    pairs = ZL * SLOTS // 2
    result = jnp.where(odd_row == lanes >> 6, shifted, partner).astype(jnp.bfloat16).reshape(pairs, 2, LANES)
    own = SLOTS // 2
    for g in range(ZH * ZL):
        z = Z_ORDER[g] % ZL
        out_ref[g * own : (g + 1) * own] = result[z * own : (z + 1) * own]
    rows.wait()


def order_kernel(data_ref, out_ref):
    own = SLOTS // 2
    halves = []
    for h in range(ZH):
        at = [Z_ORDER.index(h * ZL + z) * own for z in range(ZL)]
        halves.append(jnp.concatenate([data_ref[a : a + own] for a in at], axis=0).reshape(ZL * SLOTS, LANES))
    both = jnp.concatenate(halves, axis=1)
    rows = jnp.dot(order_matrix(), both, preferred_element_type=jnp.float32).astype(jnp.bfloat16)
    for to, (_, y, co) in enumerate(plane_order()):
        j = y * 2 + co
        for t in range(EXT_C // 2):
            for h in range(ZH):
                tile = rows[(2 * j + t) * TILE : (2 * j + t + 1) * TILE, h * LANES : (h + 1) * LANES]
                out_ref[to, (t * ZH + h) * TILE : (t * ZH + h + 1) * TILE, :] = tile


def image_kernel(data_ref, table_ref, out_ref):
    window = window_matrix()
    summed = []
    at_plane = {xyc: i for i, xyc in enumerate(plane_order())}
    for x in range(XS):
        for h in range(ZH):
            slabs = []
            for t in range(EXT_C // 2):
                at = (t * ZH + h) * TILE
                slabs.append(jnp.concatenate([data_ref[at_plane[x, j // 2, j % 2], at : at + TILE, :] for j in range(YC)], axis=0))
            summed.append(jnp.dot(window, jnp.concatenate(slabs, axis=1), preferred_element_type=jnp.float32))
    logs = []
    for t in range(EXT_C // 2):
        at = t * LANES
        columns = ([], [])
        for st in range(0, STRIPS, 2):
            a = summed[st][:, at : at + LANES]
            b = summed[st + 1][:, at : at + LANES]
            a, b = a.astype(jnp.bfloat16), b.astype(jnp.bfloat16)
            columns[0].append(jnp.concatenate([a[:, :HALF], b[:, :HALF]], axis=1))
            columns[1].append(jnp.concatenate([a[:, HALF:], b[:, HALF:]], axis=1))
        both = jnp.concatenate([jnp.concatenate(column, axis=1) for column in columns], axis=0)
        frames = lax.dot_general(table_ref[...], both, (((1,), (1,)), ((), ())), preferred_element_type=jnp.float32)
        power = frames[:EXT_R] * frames[:EXT_R] + frames[EXT_R:] * frames[EXT_R:]
        power = jnp.log(1.0 + power)
        logs += [power[:, :SUBAP], power[:, SUBAP:]]
    filtered = []
    for c in range(OWN_C):
        column = logs[c] + logs[c + 1] + logs[c + 2]
        total = column[:OWN_R] + column[1 : OWN_R + 1] + column[2 : OWN_R + 2]
        filtered.append(total * (1.0 / 9.0))
    filtered = jnp.concatenate(filtered, axis=0)
    high = filtered.astype(jnp.bfloat16)
    low = (filtered - high.astype(jnp.float32)).astype(jnp.bfloat16)
    weights = background_matrix()
    result = jnp.dot(
        jnp.concatenate([high, low], axis=1),
        jnp.concatenate([weights, weights], axis=0),
        preferred_element_type=jnp.float32,
    )
    for c in range(OWN_C):
        out_ref[:, c, :] = result[c * OWN_R : (c + 1) * OWN_R]


def body(spectra, offsets):
    strip = (lax.axis_index("x") * ZH + lax.axis_index("zh")).reshape(1)
    vmem = pl.BlockSpec(memory_space=pltpu.VMEM)
    smem = pl.BlockSpec(memory_space=pltpu.SMEM)
    hbm = pl.BlockSpec(memory_space=pltpu.HBM)
    params = pltpu.CompilerParams(vmem_limit_bytes=VMEM_BYTES)
    columns = jnp.asarray(column_matrix())
    sent, rows = pl.pallas_call(
        columns_kernel,
        out_shape=[
            jax.ShapeDtypeStruct((ZH * ZL * SLOTS // 2, 2, LANES), jnp.bfloat16),
            jax.ShapeDtypeStruct((2 * EXT_R, 2 * KR), jnp.bfloat16),
        ],
        in_specs=[smem, hbm, hbm, hbm, hbm],
        out_specs=[vmem, vmem],
        scratch_shapes=[
            pltpu.SMEM(offsets.shape, jnp.int32),
            pltpu.VMEM(spectra.shape, jnp.bfloat16),
            pltpu.VMEM(columns.shape, jnp.bfloat16),
            pltpu.SemaphoreType.DMA((5,)),
        ],
        compiler_params=params,
    )(strip, *(pltpu.with_memory_space_constraint(a, pltpu.HBM) for a in (offsets, spectra, columns, jnp.asarray(row_matrices()))))
    got = lax.all_to_all(sent.reshape(ZH * ZL, SLOTS // 2, 2, LANES), AXES, 0, 0, tiled=True, axis_index_groups=z_groups())
    sent = pl.pallas_call(
        order_kernel,
        out_shape=jax.ShapeDtypeStruct((XS * YC, EXT_C // 2 * ZH * TILE, LANES), jnp.bfloat16),
        in_specs=[vmem],
        out_specs=vmem,
        compiler_params=params,
    )(got.reshape(sent.shape))
    data = lax.all_to_all(sent, AXES, 0, 0, tiled=True, axis_index_groups=plane_groups())
    return pl.pallas_call(
        image_kernel,
        out_shape=jax.ShapeDtypeStruct((OWN_R, OWN_C, SUBAP), jnp.float32),
        in_specs=[vmem, vmem],
        out_specs=vmem,
        compiler_params=params,
    )(data, rows)


def solution(mesh):
    grid = Mesh(mesh.devices.reshape(ZL, YC // 2, 2, XS, ZH), ("zl", "y", "co", "x", "zh"))
    in_specs = (P(("zl", "y", "co"), ("x", "zh"), None), P(("zl", "y", "co")))
    out_specs = P(("x", "zh"), ("zl", "y", "co"), None)
    return jax.shard_map(body, mesh=grid, in_specs=in_specs, out_specs=out_specs, check_vma=False)
```

```python
import math

import jax
import jax.numpy as jnp
import numpy as np
import ml_dtypes
from jax import lax
from jax.experimental import pallas as pl
from jax.experimental.pallas import tpu as pltpu
from jax.sharding import Mesh, PartitionSpec as P

KR = 256
KA = 1024
ROWS = 1024
COLS = 256
WIN = 8
BG = 16
SUBAP = 128
SUBS = 64
STRIPS = 8
OWN_S = SUBAP // SUBS
OWN_K = KR // STRIPS
OWN_C = COLS // SUBS
OWN_R = ROWS // STRIPS
EXT_C = OWN_C + 2
EXT_R = OWN_R + 8
VMEM_BYTES = 24 << 20
LANES = 128
HALF = 64
ZL, YC, XS, ZH = 8, 8, 4, 2
BLOCK = COLS // ZL
PAIRS = BLOCK // 2 + 1
SLOTS = BLOCK + 2
TILE = OWN_S * ZL


def column_matrix():
    n = np.arange(KA // 2)[None, :]
    slot = np.arange(SLOTS)[None, :]
    col = (np.arange(ZL)[:, None] * BLOCK - 1 + slot).reshape(-1, 1)
    valid = np.broadcast_to(slot < BLOCK + 2, (ZL, SLOTS)).reshape(-1, 1) & (col >= 0) & (col < COLS)
    phase = ((n * col) % KA).astype(np.float64) * (2.0 * math.pi / KA)
    scale = valid / math.sqrt(KA)
    return np.stack([np.cos(phase) * scale, -np.sin(phase) * scale]).astype(ml_dtypes.bfloat16)


def row_matrices():
    scale = 1.0 / math.sqrt(KR)
    k = np.arange(KR)[None, :] - KR // 2
    out = np.zeros((STRIPS, 2, EXT_R, STRIPS, 2, OWN_K), np.float64)
    for strip in range(STRIPS):
        m = strip * OWN_R - 1 + np.arange(OWN_R + 2)
        valid = ((m >= 0) & (m < ROWS)).astype(np.float64)[:, None]
        phase = ((m[:, None] * k) % ROWS).astype(np.float64) * (2.0 * math.pi / ROWS)
        cosine = (np.cos(phase) * scale * valid).reshape(-1, STRIPS, OWN_K)
        sine = (np.sin(phase) * scale * valid).reshape(-1, STRIPS, OWN_K)
        n = OWN_R + 2
        out[strip, 0, :n, :, 0] = cosine
        out[strip, 0, :n, :, 1] = -sine
        out[strip, 1, :n, :, 0] = sine
        out[strip, 1, :n, :, 1] = cosine
    return out.reshape(STRIPS, 2 * EXT_R, 2 * KR).astype(ml_dtypes.bfloat16)


def window_matrix():
    frame = lax.broadcasted_iota(jnp.int32, (SUBAP, SUBAP), 0)
    lane = lax.broadcasted_iota(jnp.int32, (SUBAP, SUBAP), 1)
    sub = OWN_S * ((lane & (ZL - 1)) * YC + (lane >> 4)) + ((lane >> 3) & 1)
    return jnp.where(((sub - frame) & (SUBAP - 1)) < WIN, 1.0, 0.0).astype(jnp.bfloat16)


def background_matrix():
    source = lax.broadcasted_iota(jnp.int32, (SUBAP, SUBAP), 0)
    frame = lax.broadcasted_iota(jnp.int32, (SUBAP, SUBAP), 1)
    mean = jnp.where(((frame - source) & (SUBAP - 1)) < BG, 1.0 / BG, 0.0)
    return (jnp.where(source == frame, 1.0, 0.0) - mean).astype(jnp.bfloat16)


def order_matrix():
    row = lax.broadcasted_iota(jnp.int32, (PAIRS * TILE, ZL * SLOTS), 0)
    lane = lax.broadcasted_iota(jnp.int32, (PAIRS * TILE, ZL * SLOTS), 1)
    source = (row & (ZL - 1)) * SLOTS + (row >> 3)
    return jnp.where(source == lane, 1.0, 0.0).astype(jnp.bfloat16)


AXES = ("zl", "y", "co", "x", "zh")
Z_ORDER = (10, 11, 9, 12, 8, 13, 7, 14, 6, 15, 5, 0, 4, 1, 3, 2)
PLANE_ORDER = ((2, 2, 1), (2, 2, 0), (2, 3, 0), (2, 1, 0), (3, 2, 0), (1, 2, 0), (2, 0, 0), (3, 3, 0), (3, 1, 0), (0, 2, 0), (1, 3, 0), (1, 1, 0), (3, 0, 0), (0, 3, 0), (0, 1, 0), (1, 0, 0), (0, 0, 0), (2, 3, 1), (2, 1, 1), (3, 2, 1), (1, 2, 1), (2, 0, 1), (3, 3, 1), (3, 1, 1), (0, 2, 1), (1, 3, 1), (1, 1, 1), (3, 0, 1), (0, 3, 1), (0, 1, 1), (1, 0, 1), (0, 0, 1))


def place(x, y, co, z):
    zh, zl = z // ZL, z % ZL
    return (((zl * (YC // 2) + y) * 2 + co) * XS + x) * ZH + zh


def z_groups():
    return [[place(x, y, co, z) for z in Z_ORDER] for x in range(XS) for y in range(YC // 2) for co in range(2)]


def plane_order():
    return PLANE_ORDER


def plane_groups():
    return [[place(*xyc, z) for xyc in PLANE_ORDER] for z in range(ZH * ZL)]


def columns_kernel(
    strip_ref, offsets_hbm, spectra_hbm, table_hbm, tables_hbm, out_ref, rows_ref, offsets_ref, spectra_ref, table_ref, arrived
):
    small = pltpu.make_async_copy(offsets_hbm, offsets_ref, arrived.at[0])
    whole = pltpu.make_async_copy(spectra_hbm, spectra_ref, arrived.at[1])
    rows = pltpu.make_async_copy(tables_hbm.at[strip_ref[0]], rows_ref, arrived.at[2])
    fetches = [pltpu.make_async_copy(table_hbm.at[i], table_ref.at[i], arrived.at[3 + i]) for i in range(2)]
    for fetch in [small, whole] + fetches + [rows]:
        fetch.start()
    small.wait()
    lane = lax.broadcasted_iota(jnp.int32, (8, LANES), 1)
    sample = (lane & (OWN_K - 1)) + strip_ref[0] * OWN_K - KR // 2
    offset = jnp.where(lane < HALF, offsets_ref[0], offsets_ref[1])
    angle = ((offset * sample) & (ROWS - 1)).astype(jnp.float32) * (2.0 * math.pi / ROWS)
    cosine = jnp.cos(angle)[:1]
    sine = jnp.sin(angle)
    sine = jnp.where((lane & OWN_K) == 0, -sine, sine)[:1]
    whole.wait()
    re = [spectra_ref[s, :, :KA] for s in range(OWN_S)]
    im = [spectra_ref[s, :, KA:] for s in range(OWN_S)]
    mixed = None
    for fetch, part in zip(fetches, (0, 1)):
        sides = (re[0], im[0], re[1], im[1]) if part == 0 else (-im[0], re[0], -im[1], re[1])
        stack = jnp.concatenate([a[:, : KA // 2] for a in sides] + [a[:, KA // 2 :] for a in sides], axis=0)
        fetch.wait()
        product = lax.dot_general(table_ref[part], stack, (((1,), (1,)), ((), ())), preferred_element_type=jnp.float32)
        mixed = product if mixed is None else mixed + product
    odd_row = lax.broadcasted_iota(jnp.int32, (ZL * SLOTS, LANES), 0) & 1
    mixed = mixed[:, :LANES] + jnp.where(odd_row == 1, mixed[:, LANES:], -mixed[:, LANES:])
    lanes = lax.broadcasted_iota(jnp.int32, mixed.shape, 1)
    other = jnp.where((lanes & OWN_K) == 0, pltpu.roll(mixed, LANES - OWN_K, 1), pltpu.roll(mixed, OWN_K, 1))
    shifted = mixed * cosine + other * sine
    turned = pltpu.roll(shifted, HALF, 1)
    partner = jnp.where(odd_row == 1, pltpu.roll(turned, 1, 0), pltpu.roll(turned, ZL * SLOTS - 1, 0))
    pairs = ZL * SLOTS // 2
    result = jnp.where(odd_row == lanes >> 6, shifted, partner).astype(jnp.bfloat16).reshape(pairs, 2, LANES)
    own = SLOTS // 2
    for g in range(ZH * ZL):
        z = Z_ORDER[g] % ZL
        out_ref[g * own : (g + 1) * own] = result[z * own : (z + 1) * own]
    rows.wait()


def order_kernel(data_ref, out_ref):
    own = SLOTS // 2
    halves = []
    for h in range(ZH):
        at = [Z_ORDER.index(h * ZL + z) * own for z in range(ZL)]
        halves.append(jnp.concatenate([data_ref[a : a + own] for a in at], axis=0).reshape(ZL * SLOTS, LANES))
    both = jnp.concatenate(halves, axis=1)
    rows = jnp.dot(order_matrix(), both, preferred_element_type=jnp.float32).astype(jnp.bfloat16)
    for to, (_, y, co) in enumerate(plane_order()):
        j = y * 2 + co
        for t in range(EXT_C // 2):
            for h in range(ZH):
                tile = rows[(2 * j + t) * TILE : (2 * j + t + 1) * TILE, h * LANES : (h + 1) * LANES]
                out_ref[to, (t * ZH + h) * TILE : (t * ZH + h + 1) * TILE, :] = tile


def image_kernel(data_ref, table_ref, out_ref):
    window = window_matrix()
    summed = []
    at_plane = {xyc: i for i, xyc in enumerate(plane_order())}
    for x in range(XS):
        for h in range(ZH):
            slabs = []
            for t in range(EXT_C // 2):
                at = (t * ZH + h) * TILE
                slabs.append(jnp.concatenate([data_ref[at_plane[x, j // 2, j % 2], at : at + TILE, :] for j in range(YC)], axis=0))
            summed.append(jnp.dot(window, jnp.concatenate(slabs, axis=1), preferred_element_type=jnp.float32))
    logs = []
    for t in range(EXT_C // 2):
        at = t * LANES
        columns = ([], [])
        for st in range(0, STRIPS, 2):
            a = summed[st][:, at : at + LANES]
            b = summed[st + 1][:, at : at + LANES]
            a, b = a.astype(jnp.bfloat16), b.astype(jnp.bfloat16)
            columns[0].append(jnp.concatenate([a[:, :HALF], b[:, :HALF]], axis=1))
            columns[1].append(jnp.concatenate([a[:, HALF:], b[:, HALF:]], axis=1))
        both = jnp.concatenate([jnp.concatenate(column, axis=1) for column in columns], axis=0)
        frames = lax.dot_general(table_ref[...], both, (((1,), (1,)), ((), ())), preferred_element_type=jnp.float32)
        power = frames[:EXT_R] * frames[:EXT_R] + frames[EXT_R:] * frames[EXT_R:]
        power = jnp.log(1.0 + power)
        logs += [power[:, :SUBAP], power[:, SUBAP:]]
    filtered = []
    for c in range(OWN_C):
        column = logs[c] + logs[c + 1] + logs[c + 2]
        total = column[:OWN_R] + column[1 : OWN_R + 1] + column[2 : OWN_R + 2]
        filtered.append(total * (1.0 / 9.0))
    filtered = jnp.concatenate(filtered, axis=0)
    high = filtered.astype(jnp.bfloat16)
    low = (filtered - high.astype(jnp.float32)).astype(jnp.bfloat16)
    weights = background_matrix()
    result = jnp.dot(
        jnp.concatenate([high, low], axis=1),
        jnp.concatenate([weights, weights], axis=0),
        preferred_element_type=jnp.float32,
    )
    for c in range(OWN_C):
        out_ref[:, c, :] = result[c * OWN_R : (c + 1) * OWN_R]


def body(spectra, offsets):
    strip = (lax.axis_index("x") * ZH + lax.axis_index("zh")).reshape(1)
    vmem = pl.BlockSpec(memory_space=pltpu.VMEM)
    smem = pl.BlockSpec(memory_space=pltpu.SMEM)
    hbm = pl.BlockSpec(memory_space=pltpu.HBM)
    params = pltpu.CompilerParams(vmem_limit_bytes=VMEM_BYTES)
    columns = jnp.asarray(column_matrix())
    sent, rows = pl.pallas_call(
        columns_kernel,
        out_shape=[
            jax.ShapeDtypeStruct((ZH * ZL * SLOTS // 2, 2, LANES), jnp.bfloat16),
            jax.ShapeDtypeStruct((2 * EXT_R, 2 * KR), jnp.bfloat16),
        ],
        in_specs=[smem, hbm, hbm, hbm, hbm],
        out_specs=[vmem, vmem],
        scratch_shapes=[
            pltpu.SMEM(offsets.shape, jnp.int32),
            pltpu.VMEM(spectra.shape, jnp.bfloat16),
            pltpu.VMEM(columns.shape, jnp.bfloat16),
            pltpu.SemaphoreType.DMA((5,)),
        ],
        compiler_params=params,
    )(strip, *(pltpu.with_memory_space_constraint(a, pltpu.HBM) for a in (offsets, spectra, columns, jnp.asarray(row_matrices()))))
    got = lax.all_to_all(sent.reshape(ZH * ZL, SLOTS // 2, 2, LANES), AXES, 0, 0, tiled=True, axis_index_groups=z_groups())
    sent = pl.pallas_call(
        order_kernel,
        out_shape=jax.ShapeDtypeStruct((XS * YC, EXT_C // 2 * ZH * TILE, LANES), jnp.bfloat16),
        in_specs=[vmem],
        out_specs=vmem,
        compiler_params=params,
    )(got.reshape(sent.shape))
    data = lax.all_to_all(sent, AXES, 0, 0, tiled=True, axis_index_groups=plane_groups())
    return pl.pallas_call(
        image_kernel,
        out_shape=jax.ShapeDtypeStruct((OWN_R, OWN_C, SUBAP), jnp.float32),
        in_specs=[vmem, vmem],
        out_specs=vmem,
        compiler_params=params,
    )(data, rows)


def solution(mesh):
    grid = Mesh(mesh.devices.reshape(ZL, YC // 2, 2, XS, ZH), ("zl", "y", "co", "x", "zh"))
    in_specs = (P(("zl", "y", "co"), ("x", "zh"), None), P(("zl", "y", "co")))
    out_specs = P(("x", "zh"), ("zl", "y", "co"), None)
    return jax.shard_map(body, mesh=grid, in_specs=in_specs, out_specs=out_specs, check_vma=False)
```
